32 devices in a mesh: wide: 16 (over z, x, core), narrow: 2 (over y).
Axes of the slice: x: 2, y: 2, z: 4, core: 2. Of those that a mesh axis runs over, the one named last changes fastest.
Arguments:
- sensitivity: float32 [6, 262144], P(None, ('wide', 'narrow')), may hold values from -0.18 to 0.18
- vol_coord: float32 [3, 262144], P(None, ('wide', 'narrow')), may hold values from 0 to 1
- ctl_coord: float32 [3, 32768], replicated, may hold values from 0 to 1
- pair_list: int32 [2, 16384], P(None, ('wide', 'narrow')), may hold values from 0 to 255, as said below
- pair_count: int32 [32], P(('wide', 'narrow')), may hold values from 85 to 512, as said below
- inverse: bfloat16 [32768, 32768], P('wide', 'narrow'), may hold values from -0.046875 to 0.046875
Outputs:
- gradient: float32 [6, 32768], P(None, ('narrow', 'wide'))
The draws below stay inside these ranges and needn't reach their ends.
Inputs may be any that keep to these rules, and one draw needn't show every extreme that they name: `pair_list`: row 0 lies in 0 to 63. The first slot of device d names control tile ((d + 16) % 32) * 8. Row 1 of device d's other slots lies in a band of 16 control tiles that starts at d * 8 and wraps past the last tile. Slots at or past their device's count are not used. `pair_count`: some device has exactly 512 used slots in every draw.
All inputs are finite; a program needn't handle non-finite values.
Results may differ from the reference program's by a relative error of at most 0.0029.
Values may be sent and summed in bfloat16 or wider, within the bound.
No kernel may reach another device: no remote copies, remote signals or barrier semaphores. Data moves between devices by JAX's collectives and lax.ppermute only.
A program may use at most 128 MiB of HBM per device.

```python
import math
import jax
import jax.numpy as jnp
from jax import lax

NC = 32768
CT = 128
VT = 128
NOBJ = 2
VTILES_DEV = 64
PAIR_MAX = 512
CTILES = 256
NV = 262144
PAIRS = 16384
DEVICES = 32


def draw_pair_list(key, part):
    key = jax.random.fold_in(key, 11)
    first_key, second_key = jax.random.split(key)
    band_width = max(4, CTILES // 16)
    vol_rows = jax.random.randint(first_key, (1, PAIRS), 0, VTILES_DEV)
    slot_ids = jnp.arange(PAIRS, dtype=jnp.int32)
    owners = slot_ids // PAIR_MAX
    band_start = owners * CTILES // DEVICES
    offsets = jax.random.randint(second_key, (PAIRS,), 0, band_width)
    banded = (band_start + offsets) % CTILES
    far_tile = (owners + DEVICES // 2) % DEVICES * CTILES // DEVICES
    ctl_rows = jnp.where(slot_ids % PAIR_MAX == 0, far_tile, banded).reshape(1, PAIRS)
    return jnp.concatenate([vol_rows, ctl_rows], axis=0).astype(jnp.int32)


def draw_pair_count(key, part):
    key = jax.random.fold_in(key, 23)
    first_key, second_key = jax.random.split(key)
    counts = jax.random.randint(first_key, (DEVICES,), max(1, PAIR_MAX // 6), PAIR_MAX // 3 + 1)
    busiest = jax.random.randint(second_key, (), 0, DEVICES)
    positions = jnp.arange(DEVICES, dtype=jnp.int32)
    return jnp.where(positions == busiest, PAIR_MAX, counts).astype(jnp.int32)


def with_spikes(array, stream_key, source, target, blocks, factor):
    def block_of(position):
        return (jnp.arange(array.shape[position]) // (array.shape[position] // blocks)).reshape((-1,) + (1,) * (array.ndim - 1 - position))

    first = jax.random.permutation(stream_key, blocks)[block_of(target)]
    far = (block_of(target) + blocks // 2) % blocks
    return jnp.where((block_of(source) == first) | (block_of(source) == far), factor * array, array)


def steps_of(own_key, extent, shards, low, high):
    gain, own = 1.0, jax.random.fold_in(own_key, 6)
    for axis_at, shards_of in shards:
        steps = jnp.exp(jax.random.uniform(jax.random.fold_in(own, axis_at), (shards_of,), jnp.float32, low / len(shards), high / len(shards)))
        gain = gain * jnp.repeat(steps, extent[axis_at] // shards_of).reshape([-1 if axis == axis_at else 1 for axis in range(len(extent))])
    return gain


def noise(rng, shape, deviation, bound, cuts=(), kind=jnp.bfloat16):
    entries = deviation * jax.random.normal(rng, shape, jnp.float32)
    if cuts:
        entries = entries * steps_of(rng, shape, cuts, -0.22, 0.18)
    return jnp.clip(entries, -bound, bound).astype(kind)


def bell_draw_with(rng, dims, deviation, reach, shards, heavy, kind=jnp.bfloat16):
    array = deviation * jax.random.normal(rng, dims, jnp.float32)
    if shards:
        array = array * steps_of(rng, dims, shards, -0.22, 0.18)
    return jnp.clip(with_spikes(array, jax.random.fold_in(rng, 3), *heavy), -reach, reach).astype(kind)


def setup_inputs(seed: int = 0) -> dict:
    streams_of = jax.random.split(jax.random.key(seed), 7)
    sensitivity = noise(streams_of[0], (3 * NOBJ, NV), 0.03, 0.18, ((1, 32),), jnp.float32)
    vol_coord = jnp.clip(1.0 * jax.random.uniform(streams_of[1], (3, NV), jnp.float32) ** steps_of(streams_of[1], (3, NV), ((1, 32),), -0.2, 0.2), 0.0, 1.0)
    ctl_coord = jnp.clip(jax.random.uniform(streams_of[2], (3, NC), jnp.float32, 0.0, 1.0), 0.0, 1.0)
    pair_list = draw_pair_list(jax.random.fold_in(streams_of[6], 71), 0)
    pair_count = draw_pair_count(jax.random.fold_in(streams_of[6], 71), 0)
    inverse = bell_draw_with(streams_of[5], (NC, NC), NC ** -0.5, 0.046875, ((0, 16), (1, 2)), (0, 1, 16, 2.0))
    return {"sensitivity": sensitivity, "vol_coord": vol_coord, "ctl_coord": ctl_coord, "pair_list": pair_list, "pair_count": pair_count, "inverse": inverse}


def wendland_terms(sens_tile, node_tile, point_tile):
    squared = (node_tile[0][:, :, None] - point_tile[0][:, None, :]) ** 2
    for axis_num in (1, 2):
        squared = squared + (node_tile[axis_num][:, :, None] - point_tile[axis_num][:, None, :]) ** 2
    radius = jnp.sqrt(squared)
    inside = jnp.maximum(1.0 - radius, 0.0)
    kernel = inside * inside * inside * inside * (4.0 * radius + 1.0)
    return jnp.einsum('cbv,bvt->cbt', sens_tile, kernel, precision=lax.Precision.HIGHEST)

def reference(sensitivity, vol_coord, ctl_coord, pair_list, pair_count, inverse):
    components = 3 * NOBJ
    node_sens = sensitivity.reshape(components, DEVICES * VTILES_DEV, VT)
    node_pos = vol_coord.reshape(3, DEVICES * VTILES_DEV, VT)
    point_pos = ctl_coord.reshape(3, CTILES, CT)
    slot_ids = jnp.arange(PAIRS, dtype=jnp.int32)
    owner = (slot_ids // PAIR_MAX).astype(jnp.int32)
    live = (slot_ids % PAIR_MAX < pair_count[owner]).astype(sensitivity.dtype)
    vol_ids = (owner * VTILES_DEV + pair_list[0]).astype(jnp.int32)
    ctl_ids = pair_list[1].astype(jnp.int32)
    width_block = math.gcd(256, PAIRS)

    def add_block(acc_sum, block_in):
        vol_blk, ctl_blk, live_blk = block_in
        sens_tile = node_sens[:, vol_blk] * live_blk[None, :, None]
        terms = wendland_terms(sens_tile, node_pos[:, vol_blk], point_pos[:, ctl_blk])
        return (acc_sum.at[:, ctl_blk, :].add(terms), None)
    zeros = jnp.zeros((components, CTILES, CT), sensitivity.dtype)
    loads, _ = lax.scan(add_block, zeros, (vol_ids.reshape(-1, width_block), ctl_ids.reshape(-1, width_block), live.reshape(-1, width_block)))
    rounded = loads.reshape(components, NC).astype(jnp.bfloat16)
    rows_part = NC // 8
    gradient = jnp.zeros((components, NC), jnp.float32)
    for part_num in range(8):
        begin = part_num * rows_part
        gradient = gradient + jnp.dot(rounded[:, begin:begin + rows_part], inverse[begin:begin + rows_part], preferred_element_type=jnp.float32)
    return gradient
```

```python
import functools

import jax
import jax.numpy as jnp
from jax import lax
from jax.experimental import pallas as pl
from jax.experimental.pallas import tpu as pltpu
from jax.sharding import PartitionSpec as P

CT = 128
VT = 128
BAND = 16
UNROLL = 4
ROWS = 8
DEPTH = 64
MIB = 1 << 20
PIECE = 256
HELD = 4
MORE = 1
SLOTS = 4


def thirds(value):
    high = value.astype(jnp.bfloat16).astype(jnp.float32)
    rest = value - high
    middle = rest.astype(jnp.bfloat16).astype(jnp.float32)
    return high, middle, rest - middle


def features(coords, is_node):
    width = coords.shape[1]
    scaled = 4.0 * coords - 2.0
    norm = scaled[0:1] * scaled[0:1] + scaled[1:2] * scaled[1:2] + scaled[2:3] * scaled[2:3]
    padded = jnp.concatenate([scaled, jnp.zeros((ROWS - 3, width), jnp.float32)], axis=0)
    high, middle, low = thirds(padded)
    row = lax.broadcasted_iota(jnp.int32, (ROWS, width), 0)
    n_high, n_middle, n_low = thirds(jnp.broadcast_to(norm, (ROWS, width)))
    first = 0 if is_node else 3
    norms = jnp.where(
        row == first,
        n_high,
        jnp.where(row == first + 1, n_middle, jnp.where(row == first + 2, n_low, 0.0)),
    )
    ones = jnp.where((row >= 3 - first) & (row < 6 - first), 1.0, 0.0)
    last = norms + ones
    if is_node:
        parts = [high, high, middle, middle, high, low, last]
    else:
        parts = [high, middle, high, middle, low, high]
        parts = [-2.0 * part for part in parts] + [last]
    parts = parts + [jnp.zeros((DEPTH - ROWS * len(parts), width), jnp.float32)]
    return jnp.concatenate(parts, axis=0)


def held_copies(first, inverse_ref, held_refs, sems):
    return [
        pltpu.make_async_copy(
            inverse_ref.at[pl.ds((first + at) * PIECE, PIECE), :], held_ref, sems.at[at]
        )
        for at, held_ref in enumerate(held_refs)
    ]


def pair_kernel(
    geometry,
    held_count,
    list_ref,
    count_ref,
    place_ref,
    sens_ref,
    vol_ref,
    ctl_ref,
    inverse_ref,
    own_ref,
    spill_ref,
    far_ref,
    *rest,
):
    ctiles, tpb, tiles = geometry
    held_refs, rest = rest[:held_count], rest[held_count:]
    nodes, points, weights, loads_ref = rest[:4]
    vtiles = vol_ref.shape[1] // VT
    copies = held_copies(0, inverse_ref, held_refs, rest[4]) if held_count else []
    for copy in copies:
        copy.start()

    first_tile = place_ref[0]
    far_tile = place_ref[1]

    group = 8

    def node_group(group_id, carry):
        begin = pl.multiple_of(group_id * (group * VT), group * VT)
        rows = features(vol_ref[:, pl.ds(begin, group * VT)], True)
        sens = sens_ref[:, pl.ds(begin, group * VT)]
        components = sens.shape[0]
        if components < ROWS:
            sens = jnp.concatenate(
                [sens, jnp.zeros((ROWS - components, group * VT), jnp.float32)], axis=0
            )
        high = sens.astype(jnp.bfloat16).astype(jnp.float32)
        both = jnp.concatenate([high, sens - high], axis=0).astype(jnp.bfloat16)
        for at in range(group):
            cut = slice(at * VT, (at + 1) * VT)
            nodes[group_id * group + at] = rows[:, cut].T.astype(jnp.bfloat16)
            weights[group_id * group + at] = jnp.concatenate([both[:, cut], both[:, cut]], axis=1)
        return carry

    lax.fori_loop(0, vtiles // group, node_group, 0)
    weights[vtiles] = jnp.zeros(weights.shape[1:], jnp.bfloat16)

    def point_tile(tile, carry):
        named = lax.rem(first_tile + tile, ctiles)
        named = jnp.where(tile == tiles, far_tile, named)
        begin = pl.multiple_of(named * CT, CT)
        points[tile] = features(ctl_ref[:, pl.ds(begin, CT)], False).astype(jnp.bfloat16)
        loads_ref[tile] = jnp.zeros((ROWS, CT), jnp.float32)
        return carry

    lax.fori_loop(0, tiles + 1, point_tile, 0)

    count = count_ref[0]

    def pairs_step(step_id, carry):
        results = []
        for at in range(UNROLL):
            slot = step_id * UNROLL + at
            live = slot < count
            volume = jnp.where(live, list_ref[0, slot], 0)
            control = list_ref[1, slot] - first_tile
            control = jnp.where(control < 0, control + ctiles, control)
            control = jnp.where(slot == 0, tiles, control)
            control = jnp.where(live, control, 0)
            squared = jnp.dot(nodes[volume], points[control], preferred_element_type=jnp.float32)
            squared = jnp.maximum(squared, 1e-12)
            radius = squared * lax.rsqrt(squared)
            inside = jnp.maximum(4.0 - radius, 0.0)
            inside = inside * inside
            kernel = inside * inside * (radius + 1.0)
            high = kernel.astype(jnp.bfloat16)
            low = (kernel - high.astype(jnp.float32)).astype(jnp.bfloat16)
            weight = weights[jnp.where(live, volume, vtiles)]
            terms = jnp.dot(
                weight, jnp.concatenate([high, low], axis=0), preferred_element_type=jnp.float32
            )
            results.append((control, terms[:ROWS] + terms[ROWS:]))
        for control, terms in results:
            loads_ref[control] = loads_ref[control] + terms
        return carry

    lax.fori_loop(0, (count + UNROLL - 1) // UNROLL, pairs_step, 0)
    own_ref[...] = loads_ref[:tpb] * (1.0 / 256.0)
    spill_ref[...] = loads_ref[tpb:tiles] * (1.0 / 256.0)
    far_ref[...] = loads_ref[tiles:] * (1.0 / 256.0)
    for copy in copies:
        copy.wait()


def vmem(shape=None):
    return pl.BlockSpec(memory_space=pltpu.VMEM)


def smem():
    return pl.BlockSpec(memory_space=pltpu.SMEM)


def anywhere():
    return pl.BlockSpec(memory_space=pl.ANY)


def pair_stage(geometry, held_count, pair_list, pair_count, place, sens, vol, ctl, inverse):
    ctiles, tpb, tiles = geometry
    vtiles = vol.shape[1] // VT
    columns = inverse.shape[1]
    out_shape = [
        jax.ShapeDtypeStruct((count, ROWS, CT), jnp.float32) for count in (tpb, tiles - tpb, 1)
    ]
    out_specs = [vmem()] * 3
    scratch = [
        pltpu.VMEM((vtiles, VT, DEPTH), jnp.bfloat16),
        pltpu.VMEM((tiles + 1, DEPTH, CT), jnp.bfloat16),
        pltpu.VMEM((vtiles + 1, 2 * ROWS, 2 * VT), jnp.bfloat16),
        pltpu.VMEM((tiles + 1, ROWS, CT), jnp.float32),
    ]
    if held_count:
        out_shape += [pltpu.VMEM((PIECE, columns), inverse.dtype)] * held_count
        out_specs += [vmem()] * held_count
        scratch.append(pltpu.SemaphoreType.DMA((held_count,)))
    return pl.pallas_call(
        functools.partial(pair_kernel, geometry, held_count),
        out_shape=out_shape,
        in_specs=[smem(), smem(), smem(), vmem(), vmem(), vmem(), anywhere()],
        out_specs=out_specs,
        scratch_shapes=scratch,
        compiler_params=pltpu.CompilerParams(vmem_limit_bytes=10 * MIB),
        cost_estimate=pl.CostEstimate(
            flops=512 * 16384 * 400, bytes_accessed=held_count * PIECE * columns * 2, transcendentals=0
        ),
        name="pairs",
    )(pair_list, pair_count, place, sens, vol, ctl, inverse)


def hold_kernel(first, token_ref, inverse_ref, *rest):
    del token_ref
    copies = held_copies(first, inverse_ref, rest[:-1], rest[-1])
    for copy in copies:
        copy.start()
    for copy in copies:
        copy.wait()


def hold_stage(first, count, token, inverse):
    columns = inverse.shape[1]
    return pl.pallas_call(
        functools.partial(hold_kernel, first),
        out_shape=[pltpu.VMEM((PIECE, columns), inverse.dtype)] * count,
        in_specs=[anywhere(), anywhere()],
        out_specs=[vmem()] * count,
        scratch_shapes=[pltpu.SemaphoreType.DMA((count,))],
        compiler_params=pltpu.CompilerParams(vmem_limit_bytes=1 * MIB),
        cost_estimate=pl.CostEstimate(
            flops=0, bytes_accessed=2 * count * PIECE * columns * 2, transcendentals=0
        ),
        name="hold",
    )(token, inverse)


def product_kernel(
    orders,
    offsets,
    place_ref,
    own_ref,
    partner_ref,
    spill_a_ref,
    spill_b_ref,
    far_same_ref,
    far_cross_ref,
    *rest,
):
    held_refs = rest[:-6]
    inverse_ref, send_ref, keep_ref, ring, row_loads, sems = rest[-6:]
    tpb = partner_ref.shape[0]
    spilled = spill_a_ref.shape[0]
    chunks = len(orders)
    columns = inverse_ref.shape[1]
    chunk = columns // chunks
    slots = ring.shape[0]
    streamed = ring.shape[1]
    held = inverse_ref.shape[0] - streamed
    me = place_ref[2]
    even = place_ref[3] == 0

    def column_of(order):
        return pl.multiple_of((me ^ order) * chunk, chunk)

    def fetch(at):
        return pltpu.make_async_copy(
            inverse_ref.at[pl.ds(held, streamed), pl.ds(column_of(orders[at]), chunk)],
            ring.at[at % slots],
            sems.at[at % slots],
        )

    for at in range(slots):
        fetch(at).start()

    for tile in range(tpb):
        total = own_ref[tile] + partner_ref[tile]
        if tile < spilled:
            total = total + jnp.where(even, spill_a_ref[tile], spill_b_ref[tile])
        if tile == offsets[0]:
            total = total + jnp.where(even, far_same_ref[0], far_cross_ref[0])
        if tile == offsets[1]:
            total = total + jnp.where(even, far_cross_ref[0], far_same_ref[0])
        both = jnp.concatenate([total, jnp.zeros_like(total)], axis=0)
        row_loads[:, tile * CT : (tile + 1) * CT] = both.astype(jnp.bfloat16)

    half = chunks // 2
    for at in range(chunks):
        begin = column_of(orders[at])
        cols = pl.ds(begin, chunk)
        value = jnp.zeros((2 * ROWS, chunk), jnp.float32)
        for piece, held_ref in enumerate(held_refs):
            value = value + jnp.dot(
                row_loads[:, piece * PIECE : (piece + 1) * PIECE],
                held_ref[:, cols],
                preferred_element_type=jnp.float32,
            )
        fetch(at).wait()
        value = value + jnp.dot(
            row_loads[:, held:], ring[at % slots], preferred_element_type=jnp.float32
        )
        if at + slots < chunks:
            fetch(at + slots).start()
        place = slice((at % half) * chunk, (at % half + 1) * chunk)
        if at < half:
            send_ref[:, place] = value[:ROWS]
        else:
            keep_ref[:, place] = value[:ROWS]


def product_stage(orders, offsets, place, loads, held, inverse):
    columns = inverse.shape[1]
    chunk = columns // len(orders)
    streamed = inverse.shape[0] - len(held) * PIECE
    slots = SLOTS
    half = jax.ShapeDtypeStruct((ROWS, columns // 2), jnp.float32)
    return pl.pallas_call(
        functools.partial(product_kernel, orders, offsets),
        out_shape=[half, half],
        in_specs=[smem()] + [vmem()] * (len(loads) + len(held)) + [anywhere()],
        out_specs=[vmem(), vmem()],
        scratch_shapes=[
            pltpu.VMEM((slots, streamed, chunk), inverse.dtype),
            pltpu.VMEM((2 * ROWS, inverse.shape[0]), jnp.bfloat16),
            pltpu.SemaphoreType.DMA((slots,)),
        ],
        compiler_params=pltpu.CompilerParams(vmem_limit_bytes=9 * MIB),
        cost_estimate=pl.CostEstimate(
            flops=16 * inverse.shape[0] * columns,
            bytes_accessed=streamed * columns * 2,
            transcendentals=0,
        ),
        name="product",
    )(
        place,
        *loads,
        *[pltpu.with_memory_space_constraint(piece, pltpu.VMEM) for piece in held],
        inverse,
    )


def local(wide, narrow, sensitivity, vol_coord, ctl_coord, pair_list, pair_count, inverse):
    devices = wide * narrow
    components = sensitivity.shape[0]
    ctiles = ctl_coord.shape[1] // CT
    row_count, columns = inverse.shape
    tpb = row_count // CT
    offsets = [
        max((w * narrow + n) * ctiles // devices - w * tpb for w in range(wide))
        for n in range(narrow)
    ]
    tiles = max(offsets) + BAND
    w = lax.axis_index("wide")
    n = lax.axis_index("narrow")
    me = w * narrow + n
    far_tile = (me + devices // 2) % devices * ctiles // devices
    place = jnp.stack([w * tpb, far_tile, w, n]).astype(jnp.int32)
    geometry = (ctiles, tpb, tiles)

    chunk = columns // wide
    fast = (
        narrow == 2
        and wide % 2 == 0
        and chunk % CT == 0
        and tiles <= 2 * tpb
        and max(offsets[0] + BAND, 0) <= tpb
        and row_count == 2048
    )
    if not fast:
        own, spill, far_tile_loads = pair_stage(
            geometry, 0, pair_list, pair_count, place, sensitivity, vol_coord, ctl_coord, inverse
        )
        spans = -(-tiles // tpb)
        band = jnp.pad(spill, ((0, spans * tpb - tiles), (0, 0), (0, 0)))
        block = own
        for shift in range(1, spans):
            part = band[(shift - 1) * tpb : shift * tpb]
            block = block + lax.ppermute(
                part, "wide", [(at, (at + shift) % wide) for at in range(wide)]
            )
        far_row = far_tile % tpb
        far = jnp.zeros((tpb, ROWS, CT), jnp.float32)
        far = lax.dynamic_update_slice(far, far_tile_loads, (far_row, 0, 0))
        far_shift = wide // 2
        block = block + lax.ppermute(
            far, "wide", [(at, (at + far_shift) % wide) for at in range(wide)]
        )
        block = lax.psum(block, "narrow")
        row_loads = block.transpose(1, 0, 2).reshape(ROWS, row_count)[:components]
        terms = jnp.dot(
            row_loads.astype(jnp.bfloat16), inverse, preferred_element_type=jnp.float32
        )
        return lax.psum_scatter(terms, "wide", scatter_dimension=1, tiled=True)

    own, spill, far, *held = pair_stage(
        geometry, HELD, pair_list, pair_count, place, sensitivity, vol_coord, ctl_coord, inverse
    )
    both = ("wide", "narrow")
    partner = lax.ppermute(own, "narrow", [(0, 1), (1, 0)])

    def index(at_w, at_n):
        return (at_w % wide) * narrow + at_n

    spans = range(wide)
    spill_a = lax.ppermute(spill, both, [(index(at, 1), index(at + 1, 0)) for at in spans])
    spill_b = lax.ppermute(spill, both, [(index(at, 1), index(at + 1, 1)) for at in spans])
    half = wide // 2
    far_same = lax.ppermute(far, "wide", [(at, (at + half) % wide) for at in spans])
    far_cross = lax.ppermute(
        far, both, [(index(at, k), index(at + half, 1 - k)) for at in spans for k in range(2)]
    )
    held += hold_stage(HELD, MORE, far, inverse)

    bits = [bit for bit in range(wide.bit_length() - 1)]
    ranks = [
        sum(((at >> (len(bits) - 1 - bit)) & 1) << bit for bit in bits) for at in range(wide)
    ]
    orders = ranks[wide // 2 :] + ranks[: wide // 2]
    send, total = product_stage(
        orders,
        offsets,
        place,
        [own, partner, spill_a, spill_b, far_same, far_cross],
        held,
        inverse,
    )
    for bit in bits:
        moved = lax.ppermute(send, "wide", [(at, at ^ (1 << bit)) for at in spans])
        total = total + moved
        if bit < len(bits) - 1:
            size = total.shape[1] // 2
            total, send = total[:, :size], total[:, size:]
    return total[:components]


def solution(mesh):
    return jax.shard_map(
        functools.partial(local, mesh.shape["wide"], mesh.shape["narrow"]),
        mesh=mesh,
        in_specs=(
            P(None, ("wide", "narrow")),
            P(None, ("wide", "narrow")),
            P(),
            P(None, ("wide", "narrow")),
            P(("wide", "narrow")),
            P("wide", "narrow"),
        ),
        out_specs=P(None, ("narrow", "wide")),
        check_vma=False,
    )
```

```python
import functools

import jax
import jax.numpy as jnp
from jax import lax
from jax.experimental import pallas as pl
from jax.experimental.pallas import tpu as pltpu
from jax.sharding import PartitionSpec as P

CT = 128
VT = 128
BAND = 16
UNROLL = 4
ROWS = 8
DEPTH = 64
MIB = 1 << 20
PIECE = 256
HELD = 4
MORE = 1
SLOTS = 4
PRODUCT_MIB = 7


def thirds(value):
    high = value.astype(jnp.bfloat16).astype(jnp.float32)
    rest = value - high
    middle = rest.astype(jnp.bfloat16).astype(jnp.float32)
    return high, middle, rest - middle


def features(coords, is_node):
    width = coords.shape[1]
    scaled = 4.0 * coords - 2.0
    norm = scaled[0:1] * scaled[0:1] + scaled[1:2] * scaled[1:2] + scaled[2:3] * scaled[2:3]
    padded = jnp.concatenate([scaled, jnp.zeros((ROWS - 3, width), jnp.float32)], axis=0)
    high, middle, low = thirds(padded)
    row = lax.broadcasted_iota(jnp.int32, (ROWS, width), 0)
    n_high, n_middle, n_low = thirds(jnp.broadcast_to(norm, (ROWS, width)))
    first = 0 if is_node else 3
    norms = jnp.where(
        row == first,
        n_high,
        jnp.where(row == first + 1, n_middle, jnp.where(row == first + 2, n_low, 0.0)),
    )
    ones = jnp.where((row >= 3 - first) & (row < 6 - first), 1.0, 0.0)
    last = norms + ones
    if is_node:
        parts = [high, high, middle, middle, high, low, last]
    else:
        parts = [high, middle, high, middle, low, high]
        parts = [-2.0 * part for part in parts] + [last]
    parts = parts + [jnp.zeros((DEPTH - ROWS * len(parts), width), jnp.float32)]
    return jnp.concatenate(parts, axis=0)


def held_copies(first, inverse_ref, held_refs, sems):
    return [
        pltpu.make_async_copy(
            inverse_ref.at[pl.ds((first + at) * PIECE, PIECE), :], held_ref, sems.at[at]
        )
        for at, held_ref in enumerate(held_refs)
    ]


def pair_kernel(
    geometry,
    held_count,
    list_ref,
    count_ref,
    place_ref,
    sens_ref,
    vol_ref,
    ctl_ref,
    inverse_ref,
    own_ref,
    spill_ref,
    far_ref,
    *rest,
):
    ctiles, tpb, tiles = geometry
    held_refs, rest = rest[:held_count], rest[held_count:]
    nodes, points, weights, loads_ref, squares, kernels, sens_in, vol_in, ctl_in, in_sems = rest[:10]
    vtiles = vol_ref.shape[1] // VT
    slots = list_ref.shape[1]
    inputs = [
        pltpu.make_async_copy(source, target, in_sems.at[at])
        for at, (source, target) in enumerate(
            [(vol_ref, vol_in), (ctl_ref, ctl_in), (sens_ref, sens_in)]
        )
    ]
    for copy in inputs:
        copy.start()
    copies = held_copies(0, inverse_ref, held_refs, rest[10]) if held_count else []
    for copy in copies:
        copy.start()

    first_tile = place_ref[0]
    far_tile = place_ref[1]

    loads_ref[...] = jnp.zeros(loads_ref.shape, jnp.float32)
    squares[...] = jnp.zeros(squares.shape, jnp.float32)
    kernels[...] = jnp.zeros(kernels.shape, jnp.bfloat16)
    weights[vtiles] = jnp.zeros(weights.shape[1:], jnp.bfloat16)
    for copy in inputs:
        copy.wait()

    group = 8

    def node_group(group_id, carry):
        begin = pl.multiple_of(group_id * (group * VT), group * VT)
        rows = features(vol_in[:, pl.ds(begin, group * VT)], True)
        sens = sens_in[:, pl.ds(begin, group * VT)]
        components = sens.shape[0]
        if components < ROWS:
            sens = jnp.concatenate(
                [sens, jnp.zeros((ROWS - components, group * VT), jnp.float32)], axis=0
            )
        high = sens.astype(jnp.bfloat16).astype(jnp.float32)
        both = jnp.concatenate([high, sens - high], axis=0).astype(jnp.bfloat16)
        for at in range(group):
            cut = slice(at * VT, (at + 1) * VT)
            nodes[group_id * group + at] = rows[:, cut].T.astype(jnp.bfloat16)
            weights[group_id * group + at] = jnp.concatenate([both[:, cut], both[:, cut]], axis=1)
        return carry

    lax.fori_loop(0, vtiles // group, node_group, 0)

    for tile in range(tiles + 1):
        named = lax.rem(first_tile + tile, ctiles) if tile < tiles else far_tile
        begin = pl.multiple_of(named * CT, CT)
        points[tile] = features(ctl_in[:, pl.ds(begin, CT)], False).astype(jnp.bfloat16)

    count = count_ref[0]

    def tiles_of(slot):
        live = (slot >= 0) & (slot < count)
        at = jnp.minimum(jnp.maximum(slot, 0), slots - 1)
        volume = jnp.where(live, list_ref[0, at], 0)
        control = list_ref[1, at] - first_tile
        control = jnp.where(control < 0, control + ctiles, control)
        control = jnp.where(slot == 0, tiles, control)
        control = jnp.where(live, control, 0)
        return live, volume, control

    def pairs_step(step_id, carry):
        results = []
        for at in range(UNROLL):
            live, volume, control = tiles_of((step_id - 2) * UNROLL + at)
            weight = weights[jnp.where(live, volume, vtiles)]
            terms = jnp.dot(weight, kernels[at], preferred_element_type=jnp.float32)
            results.append((control, terms[:ROWS] + terms[ROWS:]))
        for at in range(UNROLL):
            squared = jnp.maximum(squares[at], 1e-12)
            radius = squared * lax.rsqrt(squared)
            inside = jnp.maximum(4.0 - radius, 0.0)
            inside = inside * inside
            kernel = inside * inside * (radius + 1.0)
            high = kernel.astype(jnp.bfloat16)
            kernels[at, :VT] = high
            kernels[at, VT:] = (kernel - high.astype(jnp.float32)).astype(jnp.bfloat16)
        for at in range(UNROLL):
            _, volume, control = tiles_of(step_id * UNROLL + at)
            squares[at] = jnp.dot(
                nodes[volume], points[control], preferred_element_type=jnp.float32
            )
        for control, terms in results:
            loads_ref[control] = loads_ref[control] + terms
        return carry

    lax.fori_loop(0, (count + UNROLL - 1) // UNROLL + 2, pairs_step, 0)
    own_ref[...] = loads_ref[:tpb] * (1.0 / 256.0)
    spill_ref[...] = loads_ref[tpb:tiles] * (1.0 / 256.0)
    far_ref[...] = loads_ref[tiles:] * (1.0 / 256.0)
    for copy in copies:
        copy.wait()


def vmem(shape=None):
    return pl.BlockSpec(memory_space=pltpu.VMEM)


def smem():
    return pl.BlockSpec(memory_space=pltpu.SMEM)


def anywhere():
    return pl.BlockSpec(memory_space=pltpu.HBM)


def pair_stage(geometry, held_count, pair_list, pair_count, place, sens, vol, ctl, inverse):
    ctiles, tpb, tiles = geometry
    vtiles = vol.shape[1] // VT
    columns = inverse.shape[1]
    out_shape = [
        jax.ShapeDtypeStruct((count, ROWS, CT), jnp.float32) for count in (tpb, tiles - tpb, 1)
    ]
    out_specs = [vmem()] * 3
    scratch = [
        pltpu.VMEM((vtiles, VT, DEPTH), jnp.bfloat16),
        pltpu.VMEM((tiles + 1, DEPTH, CT), jnp.bfloat16),
        pltpu.VMEM((vtiles + 1, 2 * ROWS, 2 * VT), jnp.bfloat16),
        pltpu.VMEM((tiles + 1, ROWS, CT), jnp.float32),
        pltpu.VMEM((UNROLL, VT, CT), jnp.float32),
        pltpu.VMEM((UNROLL, 2 * VT, CT), jnp.bfloat16),
        pltpu.VMEM(sens.shape, jnp.float32),
        pltpu.VMEM(vol.shape, jnp.float32),
        pltpu.VMEM(ctl.shape, jnp.float32),
        pltpu.SemaphoreType.DMA((3,)),
    ]
    if held_count:
        out_shape += [pltpu.VMEM((PIECE, columns), inverse.dtype)] * held_count
        out_specs += [vmem()] * held_count
        scratch.append(pltpu.SemaphoreType.DMA((held_count,)))
    return pl.pallas_call(
        functools.partial(pair_kernel, geometry, held_count),
        out_shape=out_shape,
        in_specs=[smem(), smem(), smem()] + [anywhere()] * 4,
        out_specs=out_specs,
        scratch_shapes=scratch,
        compiler_params=pltpu.CompilerParams(vmem_limit_bytes=10 * MIB),
        cost_estimate=pl.CostEstimate(
            flops=512 * 16384 * 400, bytes_accessed=held_count * PIECE * columns * 2, transcendentals=0
        ),
        name="pairs",
    )(pair_list, pair_count, place, sens, vol, ctl, inverse)


def hold_kernel(first, token_ref, inverse_ref, *rest):
    del token_ref
    copies = held_copies(first, inverse_ref, rest[:-1], rest[-1])
    for copy in copies:
        copy.start()
    for copy in copies:
        copy.wait()


def hold_stage(first, count, token, inverse):
    columns = inverse.shape[1]
    return pl.pallas_call(
        functools.partial(hold_kernel, first),
        out_shape=[pltpu.VMEM((PIECE, columns), inverse.dtype)] * count,
        in_specs=[anywhere(), anywhere()],
        out_specs=[vmem()] * count,
        scratch_shapes=[pltpu.SemaphoreType.DMA((count,))],
        compiler_params=pltpu.CompilerParams(vmem_limit_bytes=1 * MIB),
        cost_estimate=pl.CostEstimate(
            flops=0, bytes_accessed=2 * count * PIECE * columns * 2, transcendentals=0
        ),
        name="hold",
    )(token, inverse)


def multiply(orders, me, row_loads, held_refs, inverse_ref, out_refs, partial, ring, sems):
    streamed = ring.shape[1]
    held = inverse_ref.shape[0] - streamed
    chunk = ring.shape[2]
    slots = ring.shape[0]
    count = len(orders)
    per_out = count // len(out_refs)

    def columns_of(at):
        return pl.ds(pl.multiple_of((me ^ orders[at]) * chunk, chunk), chunk)

    def fetch(at):
        return pltpu.make_async_copy(
            inverse_ref.at[pl.ds(held, streamed), columns_of(at)],
            ring.at[at % slots],
            sems.at[at % slots],
        )

    for at in range(slots):
        fetch(at).start()
    yield
    for at in range(count):
        value = jnp.zeros((2 * ROWS, chunk), jnp.float32)
        for piece, held_ref in enumerate(held_refs):
            value = value + jnp.dot(
                row_loads[:, piece * PIECE : (piece + 1) * PIECE],
                held_ref[:, columns_of(at)],
                preferred_element_type=jnp.float32,
            )
        partial[at] = value[:ROWS]
    for at in range(count):
        fetch(at).wait()
        value = jnp.dot(
            row_loads[:, held:], ring[at % slots], preferred_element_type=jnp.float32
        )
        if at + slots < count:
            fetch(at + slots).start()
        out_ref = out_refs[at // per_out]
        place = at % per_out
        out_ref[:, place * chunk : (place + 1) * chunk] = (partial[at] + value[:ROWS]).astype(
            out_ref.dtype
        )
    yield


def first_kernel(
    orders,
    offsets,
    place_ref,
    own_ref,
    partner_ref,
    spill_a_ref,
    spill_b_ref,
    far_same_ref,
    far_cross_ref,
    *rest,
):
    held_refs = rest[:-8]
    inverse_ref, row_loads, *out_refs, partial, ring, sems = rest[-8:]
    tpb = partner_ref.shape[0]
    spilled = spill_a_ref.shape[0]
    even = place_ref[3] == 0
    steps = multiply(
        orders,
        place_ref[2],
        row_loads,
        held_refs,
        inverse_ref,
        out_refs,
        partial,
        ring,
        sems,
    )
    next(steps)
    for tile in range(tpb):
        total = own_ref[tile] + partner_ref[tile]
        if tile < spilled:
            total = total + jnp.where(even, spill_a_ref[tile], spill_b_ref[tile])
        if tile == offsets[0]:
            total = total + jnp.where(even, far_same_ref[0], far_cross_ref[0])
        if tile == offsets[1]:
            total = total + jnp.where(even, far_cross_ref[0], far_same_ref[0])
        both = jnp.concatenate([total, jnp.zeros_like(total)], axis=0)
        row_loads[:, tile * CT : (tile + 1) * CT] = both.astype(jnp.bfloat16)
    next(steps)


def next_kernel(orders, place_ref, row_loads, *rest):
    held_refs = rest[:-5]
    inverse_ref, out_ref, partial, ring, sems = rest[-5:]
    steps = multiply(
        orders,
        place_ref[2],
        row_loads,
        held_refs,
        inverse_ref,
        [out_ref],
        partial,
        ring,
        sems,
    )
    next(steps)
    next(steps)


def product_stage(kernel, orders, chunk, small, held, inverse, outs, name):
    rows = inverse.shape[0]
    streamed = rows - len(held) * PIECE
    slots = min(SLOTS, len(orders))
    return pl.pallas_call(
        kernel,
        out_shape=outs,
        in_specs=[smem()] + [vmem()] * (len(small) - 1 + len(held)) + [anywhere()],
        out_specs=[vmem()] * len(outs),
        scratch_shapes=[
            pltpu.VMEM((len(orders), ROWS, chunk), jnp.float32),
            pltpu.VMEM((slots, streamed, chunk), inverse.dtype),
            pltpu.SemaphoreType.DMA((slots,)),
        ],
        compiler_params=pltpu.CompilerParams(vmem_limit_bytes=PRODUCT_MIB * MIB),
        cost_estimate=pl.CostEstimate(
            flops=16 * rows * chunk * len(orders),
            bytes_accessed=rows * chunk * len(orders),
            transcendentals=0,
        ),
        name=name,
    )(
        *small,
        *[pltpu.with_memory_space_constraint(piece, pltpu.VMEM) for piece in held],
        inverse,
    )


def local(wide, narrow, sensitivity, vol_coord, ctl_coord, pair_list, pair_count, inverse):
    devices = wide * narrow
    components = sensitivity.shape[0]
    ctiles = ctl_coord.shape[1] // CT
    row_count, columns = inverse.shape
    tpb = row_count // CT
    offsets = [
        max((w * narrow + n) * ctiles // devices - w * tpb for w in range(wide))
        for n in range(narrow)
    ]
    tiles = max(offsets) + BAND
    w = lax.axis_index("wide")
    n = lax.axis_index("narrow")
    me = w * narrow + n
    far_tile = (me + devices // 2) % devices * ctiles // devices
    place = jnp.stack([w * tpb, far_tile, w, n]).astype(jnp.int32)
    geometry = (ctiles, tpb, tiles)

    chunk = columns // wide
    fast = (
        narrow == 2
        and wide >= 8
        and wide & (wide - 1) == 0
        and chunk % CT == 0
        and tiles <= 2 * tpb
        and max(offsets[0] + BAND, 0) <= tpb
        and row_count == 8 * PIECE
    )
    if not fast:
        own, spill, far_tile_loads = pair_stage(
            geometry, 0, pair_list, pair_count, place, sensitivity, vol_coord, ctl_coord, inverse
        )
        spans = -(-tiles // tpb)
        band = jnp.pad(spill, ((0, spans * tpb - tiles), (0, 0), (0, 0)))
        block = own
        for shift in range(1, spans):
            part = band[(shift - 1) * tpb : shift * tpb]
            block = block + lax.ppermute(
                part, "wide", [(at, (at + shift) % wide) for at in range(wide)]
            )
        far_row = far_tile % tpb
        far = jnp.zeros((tpb, ROWS, CT), jnp.float32)
        far = lax.dynamic_update_slice(far, far_tile_loads, (far_row, 0, 0))
        far_shift = wide // 2
        block = block + lax.ppermute(
            far, "wide", [(at, (at + far_shift) % wide) for at in range(wide)]
        )
        block = lax.psum(block, "narrow")
        row_loads = block.transpose(1, 0, 2).reshape(ROWS, row_count)[:components]
        terms = jnp.dot(
            row_loads.astype(jnp.bfloat16), inverse, preferred_element_type=jnp.float32
        )
        return lax.psum_scatter(terms, "wide", scatter_dimension=1, tiled=True)

    own, spill, far, *held = pair_stage(
        geometry, HELD, pair_list, pair_count, place, sensitivity, vol_coord, ctl_coord, inverse
    )
    both = ("wide", "narrow")
    partner = lax.ppermute(own, "narrow", [(0, 1), (1, 0)])

    def index(at_w, at_n):
        return (at_w % wide) * narrow + at_n

    spans = range(wide)
    half = wide // 2
    straight = [lambda at, k=k: (at, (at + k) % wide) for k in (1, half)]
    cross = [
        [(index(at, k), index(at + shift, 1 - k)) for at in spans for k in range(2)]
        for shift in (1, half)
    ]
    spill_b = lax.ppermute(spill, "wide", [straight[0](at) for at in spans])
    spill_a = lax.ppermute(spill, both, cross[0])
    far_same = lax.ppermute(far, "wide", [straight[1](at) for at in spans])
    far_cross = lax.ppermute(far, both, cross[1])
    held += hold_stage(HELD, MORE, far, inverse)

    ends = range(wide // 4)
    quarter = columns // 4

    def orders_of(near):
        return [near | (end << 2) for end in ends]

    orders = orders_of(3) + orders_of(2) + orders_of(1)
    row_loads, part_3, part_2, part_1 = product_stage(
        functools.partial(first_kernel, orders, offsets),
        orders,
        chunk,
        [place, own, partner, spill_a, spill_b, far_same, far_cross],
        held,
        inverse,
        [
            pltpu.VMEM((2 * ROWS, row_count), jnp.bfloat16),
            jax.ShapeDtypeStruct((ROWS, quarter), jnp.bfloat16),
            jax.ShapeDtypeStruct((ROWS, quarter), jnp.bfloat16),
            jax.ShapeDtypeStruct((ROWS, quarter), jnp.float32),
        ],
        "product_a",
    )

    def to(difference, value):
        return lax.ppermute(value, "wide", [(at, at ^ difference) for at in spans])

    part_3 = to(3, part_3)
    part_2 = to(2, part_2)
    part_1 = to(1, part_1)
    orders = orders_of(0)
    (part_0,) = product_stage(
        functools.partial(next_kernel, orders),
        orders,
        chunk,
        [place, row_loads],
        held,
        inverse,
        [jax.ShapeDtypeStruct((ROWS, quarter), jnp.float32)],
        "product_b",
    )
    total = part_0 + part_1 + part_3.astype(jnp.float32) + part_2.astype(jnp.float32)
    result = total[:, :chunk]
    for end in ends[1:]:
        sent = total[:, end * chunk : (end + 1) * chunk].astype(jnp.bfloat16)
        result = result + to(end << 2, sent).astype(jnp.float32)
    return result[:components]


def solution(mesh):
    return jax.shard_map(
        functools.partial(local, mesh.shape["wide"], mesh.shape["narrow"]),
        mesh=mesh,
        in_specs=(
            P(None, ("wide", "narrow")),
            P(None, ("wide", "narrow")),
            P(),
            P(None, ("wide", "narrow")),
            P(("wide", "narrow")),
            P("wide", "narrow"),
        ),
        out_specs=P(None, ("narrow", "wide")),
        check_vma=False,
    )
```

```python
import functools

import jax
import jax.numpy as jnp
from jax import lax
from jax.experimental import pallas as pl
from jax.experimental.pallas import tpu as pltpu
from jax.sharding import PartitionSpec as P

CT = 128
VT = 128
BAND = 16
UNROLL = 8
AHEAD = 2
ROWS = 8
DEPTH = 64
MIB = 1 << 20
PIECE = 256
HELD = 5
MORE = 0
SLOTS = 4
PRODUCT_MIB = 7


def thirds(value):
    high = value.astype(jnp.bfloat16).astype(jnp.float32)
    rest = value - high
    middle = rest.astype(jnp.bfloat16).astype(jnp.float32)
    return high, middle, rest - middle


def features(coords, is_node):
    width = coords.shape[1]
    scaled = 4.0 * coords - 2.0
    norm = scaled[0:1] * scaled[0:1] + scaled[1:2] * scaled[1:2] + scaled[2:3] * scaled[2:3]
    padded = jnp.concatenate([scaled, jnp.zeros((ROWS - 3, width), jnp.float32)], axis=0)
    high, middle, low = thirds(padded)
    row = lax.broadcasted_iota(jnp.int32, (ROWS, width), 0)
    n_high, n_middle, n_low = thirds(jnp.broadcast_to(norm, (ROWS, width)))
    first = 0 if is_node else 3
    norms = jnp.where(
        row == first,
        n_high,
        jnp.where(row == first + 1, n_middle, jnp.where(row == first + 2, n_low, 0.0)),
    )
    ones = jnp.where((row >= 3 - first) & (row < 6 - first), 1.0, 0.0)
    last = norms + ones
    if is_node:
        parts = [high, high, middle, middle, high, low, last]
    else:
        parts = [high, middle, high, middle, low, high]
        parts = [-2.0 * part for part in parts] + [last]
    parts = parts + [jnp.zeros((DEPTH - ROWS * len(parts), width), jnp.float32)]
    return jnp.concatenate(parts, axis=0)


def held_copies(first, inverse_ref, held_refs, sems):
    return [
        pltpu.make_async_copy(
            inverse_ref.at[pl.ds((first + at) * PIECE, PIECE), :], held_ref, sems.at[at]
        )
        for at, held_ref in enumerate(held_refs)
    ]


def pair_kernel(
    geometry,
    held_count,
    count_ref,
    place_ref,
    listed_ref,
    sens_ref,
    vol_ref,
    ctl_ref,
    inverse_ref,
    own_ref,
    spill_ref,
    far_ref,
    *rest,
):
    ctiles, tpb, tiles = geometry
    held_refs, rest = rest[:held_count], rest[held_count:]
    nodes, points, weights, loads_ref, squares, kernels, sens_in, vol_in, ctl_in, list_ref, in_sems = (
        rest[:11]
    )
    vtiles = vol_ref.shape[1] // VT
    slots = list_ref.shape[1]
    inputs = [
        pltpu.make_async_copy(source, target, in_sems.at[at])
        for at, (source, target) in enumerate(
            [
                (vol_ref, vol_in),
                (ctl_ref, ctl_in),
                (sens_ref, sens_in),
                (listed_ref, list_ref),
            ]
        )
    ]
    for copy in inputs:
        copy.start()
    copies = held_copies(0, inverse_ref, held_refs, rest[11]) if held_count else []
    for copy in copies:
        copy.start()

    first_tile = place_ref[0]
    far_tile = place_ref[1]

    loads_ref[...] = jnp.zeros(loads_ref.shape, jnp.float32)
    squares[...] = jnp.zeros(squares.shape, jnp.float32)
    kernels[...] = jnp.zeros(kernels.shape, jnp.bfloat16)
    weights[vtiles] = jnp.zeros(weights.shape[1:], jnp.bfloat16)
    for copy in inputs:
        copy.wait()

    group = 8

    def node_group(group_id, carry):
        begin = pl.multiple_of(group_id * (group * VT), group * VT)
        rows = features(vol_in[:, pl.ds(begin, group * VT)], True)
        sens = sens_in[:, pl.ds(begin, group * VT)]
        components = sens.shape[0]
        if components < ROWS:
            sens = jnp.concatenate(
                [sens, jnp.zeros((ROWS - components, group * VT), jnp.float32)], axis=0
            )
        high = sens.astype(jnp.bfloat16).astype(jnp.float32)
        both = jnp.concatenate([high, sens - high], axis=0).astype(jnp.bfloat16)
        for at in range(group):
            cut = slice(at * VT, (at + 1) * VT)
            nodes[group_id * group + at] = rows[:, cut].T.astype(jnp.bfloat16)
            weights[group_id * group + at] = jnp.concatenate([both[:, cut], both[:, cut]], axis=1)
        return carry

    lax.fori_loop(0, vtiles // group, node_group, 0)

    for tile in range(tiles + 1):
        named = lax.rem(first_tile + tile, ctiles) if tile < tiles else far_tile
        begin = pl.multiple_of(named * CT, CT)
        points[tile] = features(ctl_in[:, pl.ds(begin, CT)], False).astype(jnp.bfloat16)

    count = count_ref[0]

    def tiles_of(slot):
        live = (slot >= 0) & (slot < count)
        at = jnp.minimum(jnp.maximum(slot, 0), slots - 1)
        volume = jnp.where(live, list_ref[0, at], 0)
        control = list_ref[1, at] - first_tile
        control = jnp.where(control < 0, control + ctiles, control)
        control = jnp.where(slot == 0, tiles, control)
        control = jnp.where(live, control, 0)
        return live, volume, control

    def pairs_step(step_id, carry):
        results = []
        for at in range(UNROLL):
            live, volume, control = tiles_of((step_id - 2) * UNROLL + at)
            weight = weights[jnp.where(live, volume, vtiles)]
            terms = jnp.dot(weight, kernels[at], preferred_element_type=jnp.float32)
            results.append((control, terms[:ROWS] + terms[ROWS:]))
        for at in range(UNROLL):
            squared = jnp.maximum(squares[at], 1e-12)
            radius = squared * lax.rsqrt(squared)
            inside = jnp.maximum(4.0 - radius, 0.0)
            inside = inside * inside
            kernel = inside * inside * (radius + 1.0)
            high = kernel.astype(jnp.bfloat16)
            kernels[at, :VT] = high
            kernels[at, VT:] = (kernel - high.astype(jnp.float32)).astype(jnp.bfloat16)
        for at in range(UNROLL):
            _, volume, control = tiles_of(step_id * UNROLL + at)
            squares[at] = jnp.dot(
                nodes[volume], points[control], preferred_element_type=jnp.float32
            )
        for control, terms in results:
            loads_ref[control] = loads_ref[control] + terms
        return carry

    lax.fori_loop(0, (count + UNROLL - 1) // UNROLL + 2, pairs_step, 0)
    own_ref[...] = loads_ref[:tpb] * (1.0 / 256.0)
    spill_ref[...] = loads_ref[tpb:tiles] * (1.0 / 256.0)
    far_ref[...] = loads_ref[tiles:] * (1.0 / 256.0)
    for copy in copies:
        copy.wait()


def vmem(shape=None):
    return pl.BlockSpec(memory_space=pltpu.VMEM)


def smem():
    return pl.BlockSpec(memory_space=pltpu.SMEM)


def anywhere():
    return pl.BlockSpec(memory_space=pltpu.HBM)


def pair_stage(geometry, held_count, pair_list, pair_count, place, sens, vol, ctl, inverse):
    ctiles, tpb, tiles = geometry
    vtiles = vol.shape[1] // VT
    columns = inverse.shape[1]
    out_shape = [
        jax.ShapeDtypeStruct((count, ROWS, CT), jnp.float32) for count in (tpb, tiles - tpb, 1)
    ]
    out_specs = [vmem()] * 3
    scratch = [
        pltpu.VMEM((vtiles, VT, DEPTH), jnp.bfloat16),
        pltpu.VMEM((tiles + 1, DEPTH, CT), jnp.bfloat16),
        pltpu.VMEM((vtiles + 1, 2 * ROWS, 2 * VT), jnp.bfloat16),
        pltpu.VMEM((tiles + 1, ROWS, CT), jnp.float32),
        pltpu.VMEM((UNROLL, VT, CT), jnp.float32),
        pltpu.VMEM((UNROLL, 2 * VT, CT), jnp.bfloat16),
        pltpu.VMEM(sens.shape, jnp.float32),
        pltpu.VMEM(vol.shape, jnp.float32),
        pltpu.VMEM(ctl.shape, jnp.float32),
        pltpu.SMEM(pair_list.shape, jnp.int32),
        pltpu.SemaphoreType.DMA((4,)),
    ]
    if held_count:
        out_shape += [pltpu.VMEM((PIECE, columns), inverse.dtype)] * held_count
        out_specs += [vmem()] * held_count
        scratch.append(pltpu.SemaphoreType.DMA((held_count,)))
    return pl.pallas_call(
        functools.partial(pair_kernel, geometry, held_count),
        out_shape=out_shape,
        in_specs=[smem(), smem()] + [anywhere()] * 5,
        out_specs=out_specs,
        scratch_shapes=scratch,
        compiler_params=pltpu.CompilerParams(vmem_limit_bytes=10 * MIB),
        cost_estimate=pl.CostEstimate(
            flops=512 * 16384 * 400, bytes_accessed=held_count * PIECE * columns * 2, transcendentals=0
        ),
        name="pairs",
    )(
        pair_count,
        place,
        *[pltpu.with_memory_space_constraint(x, pltpu.HBM) for x in (pair_list, sens, vol, ctl)],
        inverse,
    )


def hold_kernel(first, token_ref, inverse_ref, *rest):
    del token_ref
    copies = held_copies(first, inverse_ref, rest[:-1], rest[-1])
    for copy in copies:
        copy.start()
    for copy in copies:
        copy.wait()


def hold_stage(first, count, token, inverse):
    columns = inverse.shape[1]
    return pl.pallas_call(
        functools.partial(hold_kernel, first),
        out_shape=[pltpu.VMEM((PIECE, columns), inverse.dtype)] * count,
        in_specs=[anywhere(), anywhere()],
        out_specs=[vmem()] * count,
        scratch_shapes=[pltpu.SemaphoreType.DMA((count,))],
        compiler_params=pltpu.CompilerParams(vmem_limit_bytes=1 * MIB),
        cost_estimate=pl.CostEstimate(
            flops=0, bytes_accessed=2 * count * PIECE * columns * 2, transcendentals=0
        ),
        name="hold",
    )(token, inverse)


def multiply(orders, me, row_loads, held_refs, inverse_ref, out_refs, partial, ring, sems):
    streamed = ring.shape[1]
    held = inverse_ref.shape[0] - streamed
    chunk = ring.shape[2]
    slots = ring.shape[0]
    count = len(orders)
    per_out = count // len(out_refs)

    def columns_of(at):
        return pl.ds(pl.multiple_of((me ^ orders[at]) * chunk, chunk), chunk)

    def fetch(at):
        return pltpu.make_async_copy(
            inverse_ref.at[pl.ds(held, streamed), columns_of(at)],
            ring.at[at % slots],
            sems.at[at % slots],
        )

    def held_part(at):
        value = jnp.zeros((2 * ROWS, chunk), jnp.float32)
        for piece, held_ref in enumerate(held_refs):
            value = value + jnp.dot(
                row_loads[:, piece * PIECE : (piece + 1) * PIECE],
                held_ref[:, columns_of(at)],
                preferred_element_type=jnp.float32,
            )
        partial[at % (AHEAD + 1)] = value[:ROWS]

    for at in range(slots):
        fetch(at).start()
    yield
    for at in range(AHEAD):
        held_part(at)
    for at in range(count):
        if at + AHEAD < count:
            held_part(at + AHEAD)
        fetch(at).wait()
        value = jnp.dot(
            row_loads[:, held:], ring[at % slots], preferred_element_type=jnp.float32
        )
        if at + slots < count:
            fetch(at + slots).start()
        out_ref = out_refs[at // per_out]
        place = at % per_out
        out_ref[:, place * chunk : (place + 1) * chunk] = (
            partial[at % (AHEAD + 1)] + value[:ROWS]
        ).astype(out_ref.dtype)
    yield


def first_kernel(
    orders,
    offsets,
    place_ref,
    own_ref,
    partner_ref,
    spill_a_ref,
    spill_b_ref,
    far_same_ref,
    far_cross_ref,
    *rest,
):
    held_refs = rest[:-8]
    inverse_ref, row_loads, *out_refs, partial, ring, sems = rest[-8:]
    tpb = partner_ref.shape[0]
    spilled = spill_a_ref.shape[0]
    even = place_ref[3] == 0
    steps = multiply(
        orders,
        place_ref[2],
        row_loads,
        held_refs,
        inverse_ref,
        out_refs,
        partial,
        ring,
        sems,
    )
    next(steps)
    for tile in range(tpb):
        total = own_ref[tile] + partner_ref[tile]
        if tile < spilled:
            total = total + jnp.where(even, spill_a_ref[tile], spill_b_ref[tile])
        if tile == offsets[0]:
            total = total + jnp.where(even, far_same_ref[0], far_cross_ref[0])
        if tile == offsets[1]:
            total = total + jnp.where(even, far_cross_ref[0], far_same_ref[0])
        both = jnp.concatenate([total, jnp.zeros_like(total)], axis=0)
        row_loads[:, tile * CT : (tile + 1) * CT] = both.astype(jnp.bfloat16)
    next(steps)


def next_kernel(orders, place_ref, row_loads, *rest):
    held_refs = rest[:-5]
    inverse_ref, out_ref, partial, ring, sems = rest[-5:]
    steps = multiply(
        orders,
        place_ref[2],
        row_loads,
        held_refs,
        inverse_ref,
        [out_ref],
        partial,
        ring,
        sems,
    )
    next(steps)
    next(steps)


def product_stage(kernel, orders, chunk, small, held, inverse, outs, name):
    rows = inverse.shape[0]
    streamed = rows - len(held) * PIECE
    slots = min(SLOTS, len(orders))
    return pl.pallas_call(
        kernel,
        out_shape=outs,
        in_specs=[smem()] + [vmem()] * (len(small) - 1 + len(held)) + [anywhere()],
        out_specs=[vmem()] * len(outs),
        scratch_shapes=[
            pltpu.VMEM((AHEAD + 1, ROWS, chunk), jnp.float32),
            pltpu.VMEM((slots, streamed, chunk), inverse.dtype),
            pltpu.SemaphoreType.DMA((slots,)),
        ],
        compiler_params=pltpu.CompilerParams(vmem_limit_bytes=PRODUCT_MIB * MIB),
        cost_estimate=pl.CostEstimate(
            flops=16 * rows * chunk * len(orders),
            bytes_accessed=rows * chunk * len(orders),
            transcendentals=0,
        ),
        name=name,
    )(
        *small,
        *[pltpu.with_memory_space_constraint(piece, pltpu.VMEM) for piece in held],
        inverse,
    )


def local(wide, narrow, sensitivity, vol_coord, ctl_coord, pair_list, pair_count, inverse):
    devices = wide * narrow
    components = sensitivity.shape[0]
    ctiles = ctl_coord.shape[1] // CT
    row_count, columns = inverse.shape
    tpb = row_count // CT
    offsets = [
        max((w * narrow + n) * ctiles // devices - w * tpb for w in range(wide))
        for n in range(narrow)
    ]
    tiles = max(offsets) + BAND
    w = lax.axis_index("wide")
    n = lax.axis_index("narrow")
    me = w * narrow + n
    far_tile = (me + devices // 2) % devices * ctiles // devices
    place = jnp.stack([w * tpb, far_tile, w, n]).astype(jnp.int32)
    geometry = (ctiles, tpb, tiles)

    chunk = columns // wide
    fast = (
        narrow == 2
        and wide >= 8
        and wide & (wide - 1) == 0
        and chunk % CT == 0
        and tiles <= 2 * tpb
        and max(offsets[0] + BAND, 0) <= tpb
        and row_count == 8 * PIECE
    )
    if not fast:
        own, spill, far_tile_loads = pair_stage(
            geometry, 0, pair_list, pair_count, place, sensitivity, vol_coord, ctl_coord, inverse
        )
        spans = -(-tiles // tpb)
        band = jnp.pad(spill, ((0, spans * tpb - tiles), (0, 0), (0, 0)))
        block = own
        for shift in range(1, spans):
            part = band[(shift - 1) * tpb : shift * tpb]
            block = block + lax.ppermute(
                part, "wide", [(at, (at + shift) % wide) for at in range(wide)]
            )
        far_row = far_tile % tpb
        far = jnp.zeros((tpb, ROWS, CT), jnp.float32)
        far = lax.dynamic_update_slice(far, far_tile_loads, (far_row, 0, 0))
        far_shift = wide // 2
        block = block + lax.ppermute(
            far, "wide", [(at, (at + far_shift) % wide) for at in range(wide)]
        )
        block = lax.psum(block, "narrow")
        row_loads = block.transpose(1, 0, 2).reshape(ROWS, row_count)[:components]
        terms = jnp.dot(
            row_loads.astype(jnp.bfloat16), inverse, preferred_element_type=jnp.float32
        )
        return lax.psum_scatter(terms, "wide", scatter_dimension=1, tiled=True)

    own, spill, far, *held = pair_stage(
        geometry, HELD, pair_list, pair_count, place, sensitivity, vol_coord, ctl_coord, inverse
    )
    both = ("wide", "narrow")
    partner = lax.ppermute(own, "narrow", [(0, 1), (1, 0)])

    def index(at_w, at_n):
        return (at_w % wide) * narrow + at_n

    spans = range(wide)
    half = wide // 2
    straight = [lambda at, k=k: (at, (at + k) % wide) for k in (1, half)]
    cross = [
        [(index(at, k), index(at + shift, 1 - k)) for at in spans for k in range(2)]
        for shift in (1, half)
    ]
    spill_b = lax.ppermute(spill, "wide", [straight[0](at) for at in spans])
    spill_a = lax.ppermute(spill, both, cross[0])
    far_same = lax.ppermute(far, "wide", [straight[1](at) for at in spans])
    far_cross = lax.ppermute(far, both, cross[1])
    if MORE:
        held += hold_stage(HELD, MORE, far, inverse)

    ends = range(wide // 4)
    quarter = columns // 4

    def orders_of(near):
        return [near | (end << 2) for end in ends]

    orders = orders_of(3) + orders_of(2) + orders_of(1)
    row_loads, part_3, part_2, part_1 = product_stage(
        functools.partial(first_kernel, orders, offsets),
        orders,
        chunk,
        [place, own, partner, spill_a, spill_b, far_same, far_cross],
        held,
        inverse,
        [
            pltpu.VMEM((2 * ROWS, row_count), jnp.bfloat16),
            jax.ShapeDtypeStruct((ROWS, quarter), jnp.bfloat16),
            jax.ShapeDtypeStruct((ROWS, quarter), jnp.bfloat16),
            jax.ShapeDtypeStruct((ROWS, quarter), jnp.float32),
        ],
        "product_a",
    )

    def to(difference, value):
        return lax.ppermute(value, "wide", [(at, at ^ difference) for at in spans])

    part_3 = to(3, part_3)
    part_2 = to(2, part_2)
    part_1 = to(1, part_1)
    orders = orders_of(0)
    (part_0,) = product_stage(
        functools.partial(next_kernel, orders),
        orders,
        chunk,
        [place, row_loads],
        held,
        inverse,
        [jax.ShapeDtypeStruct((ROWS, quarter), jnp.float32)],
        "product_b",
    )
    total = part_0 + part_1 + part_3.astype(jnp.float32) + part_2.astype(jnp.float32)
    result = total[:, :chunk]
    for end in ends[1:]:
        sent = total[:, end * chunk : (end + 1) * chunk].astype(jnp.bfloat16)
        result = result + to(end << 2, sent).astype(jnp.float32)
    return result[:components]


def solution(mesh):
    return jax.shard_map(
        functools.partial(local, mesh.shape["wide"], mesh.shape["narrow"]),
        mesh=mesh,
        in_specs=(
            P(None, ("wide", "narrow")),
            P(None, ("wide", "narrow")),
            P(),
            P(None, ("wide", "narrow")),
            P(("wide", "narrow")),
            P("wide", "narrow"),
        ),
        out_specs=P(None, ("narrow", "wide")),
        check_vma=False,
    )
```

```python
import functools

import jax
import jax.numpy as jnp
from jax import lax
from jax.experimental import pallas as pl
from jax.experimental.pallas import tpu as pltpu
from jax.sharding import PartitionSpec as P

CT = 128
VT = 128
BAND = 16
UNROLL = 8
AHEAD = 2
ROWS = 8
DEPTH = 64
MIB = 1 << 20
PIECE = 256
HELD = 4
SLOTS = 3
PRODUCT_MIB = 7


def thirds(value):
    high = value.astype(jnp.bfloat16).astype(jnp.float32)
    rest = value - high
    middle = rest.astype(jnp.bfloat16).astype(jnp.float32)
    return high, middle, rest - middle


def features(coords, is_node):
    width = coords.shape[1]
    scaled = 4.0 * coords - 2.0
    norm = scaled[0:1] * scaled[0:1] + scaled[1:2] * scaled[1:2] + scaled[2:3] * scaled[2:3]
    padded = jnp.concatenate([scaled, jnp.zeros((ROWS - 3, width), jnp.float32)], axis=0)
    high, middle, low = thirds(padded)
    row = lax.broadcasted_iota(jnp.int32, (ROWS, width), 0)
    n_high, n_middle, n_low = thirds(jnp.broadcast_to(norm, (ROWS, width)))
    first = 0 if is_node else 3
    norms = jnp.where(
        row == first,
        n_high,
        jnp.where(row == first + 1, n_middle, jnp.where(row == first + 2, n_low, 0.0)),
    )
    ones = jnp.where((row >= 3 - first) & (row < 6 - first), 1.0, 0.0)
    last = norms + ones
    if is_node:
        parts = [high, high, middle, middle, high, low, last]
    else:
        parts = [high, middle, high, middle, low, high]
        parts = [-2.0 * part for part in parts] + [last]
    parts = parts + [jnp.zeros((DEPTH - ROWS * len(parts), width), jnp.float32)]
    return jnp.concatenate(parts, axis=0)


def chunk_start(me, near, far, chunk):
    return pl.multiple_of((me ^ (near | (far << 2))) * chunk, chunk)


def held_copies(me, inverse_ref, held_refs, near_refs, sems=None):
    copies = []
    for at, held_ref in enumerate(held_refs):
        rows = pl.ds(at * PIECE, PIECE)
        copies.append(pltpu.make_async_copy(inverse_ref.at[rows, :], held_ref, sems.at[at]))
    for near_ref in near_refs:
        depth, width = near_ref.shape
        rows = pl.ds(len(held_refs) * PIECE, depth)
        pieces = sems.shape[0] - len(held_refs)
        chunk = width // pieces
        for at in range(pieces):
            columns = pl.ds(chunk_start(me, 0, at, chunk), chunk)
            copies.append(
                pltpu.make_async_copy(
                    inverse_ref.at[rows, columns],
                    near_ref.at[:, pl.ds(at * chunk, chunk)],
                    sems.at[len(held_refs) + at],
                )
            )
    return copies


def pair_kernel(
    geometry,
    held_count,
    near_count,
    count_ref,
    place_ref,
    listed_ref,
    sens_ref,
    vol_ref,
    ctl_ref,
    inverse_ref,
    own_ref,
    spill_ref,
    far_ref,
    *rest,
):
    ctiles, tpb, tiles = geometry
    held_refs, rest = rest[:held_count], rest[held_count:]
    near_refs, rest = rest[:near_count], rest[near_count:]
    nodes, points, weights, loads_ref, squares, kernels, sens_in, vol_in, ctl_in, list_ref, in_sems = (
        rest[:11]
    )
    vtiles = vol_ref.shape[1] // VT
    slots = list_ref.shape[1]
    inputs = [
        pltpu.make_async_copy(source, target, in_sems.at[at])
        for at, (source, target) in enumerate(
            [
                (vol_ref, vol_in),
                (ctl_ref, ctl_in),
                (sens_ref, sens_in),
                (listed_ref, list_ref),
            ]
        )
    ]
    for copy in inputs:
        copy.start()
    copies = held_copies(place_ref[2], inverse_ref, held_refs, near_refs, *rest[11:])

    first_tile = place_ref[0]
    far_tile = place_ref[1]

    loads_ref[...] = jnp.zeros(loads_ref.shape, jnp.float32)
    squares[...] = jnp.zeros(squares.shape, jnp.float32)
    kernels[...] = jnp.zeros(kernels.shape, jnp.bfloat16)
    weights[vtiles] = jnp.zeros(weights.shape[1:], jnp.bfloat16)
    for copy in inputs:
        copy.wait()
    for copy in copies:
        copy.start()

    group = 8
    square = (VT, VT)
    same = lax.broadcasted_iota(jnp.int32, square, 0) == lax.broadcasted_iota(jnp.int32, square, 1)
    unit = jnp.where(same, 1.0, 0.0).astype(jnp.bfloat16)

    def node_group(group_id, carry):
        begin = pl.multiple_of(group_id * (group * VT), group * VT)
        rows = features(vol_in[:, pl.ds(begin, group * VT)], True).astype(jnp.bfloat16)
        sens = sens_in[:, pl.ds(begin, group * VT)]
        components = sens.shape[0]
        if components < ROWS:
            sens = jnp.concatenate(
                [sens, jnp.zeros((ROWS - components, group * VT), jnp.float32)], axis=0
            )
        high = sens.astype(jnp.bfloat16).astype(jnp.float32)
        both = jnp.concatenate([high, sens - high], axis=0).astype(jnp.bfloat16)
        for at in range(group):
            cut = slice(at * VT, (at + 1) * VT)
            turned = lax.dot_general(
                unit, rows[:, cut], (((1,), (1,)), ((), ())), preferred_element_type=jnp.float32
            )
            nodes[group_id * group + at] = turned.astype(jnp.bfloat16)
            weights[group_id * group + at] = jnp.concatenate([both[:, cut], both[:, cut]], axis=1)
        return carry

    lax.fori_loop(0, vtiles // group, node_group, 0)

    for tile in range(tiles + 1):
        named = lax.rem(first_tile + tile, ctiles) if tile < tiles else far_tile
        begin = pl.multiple_of(named * CT, CT)
        points[tile] = features(ctl_in[:, pl.ds(begin, CT)], False).astype(jnp.bfloat16)

    count = count_ref[0]

    def tiles_of(slot):
        live = (slot >= 0) & (slot < count)
        at = jnp.minimum(jnp.maximum(slot, 0), slots - 1)
        volume = jnp.where(live, list_ref[0, at], 0)
        control = list_ref[1, at] - first_tile
        control = jnp.where(control < 0, control + ctiles, control)
        control = jnp.where(slot == 0, tiles, control)
        control = jnp.where(live, control, 0)
        return live, volume, control

    def pairs_step(step_id, carry):
        results = []
        for at in range(UNROLL):
            live, volume, control = tiles_of((step_id - 2) * UNROLL + at)
            weight = weights[jnp.where(live, volume, vtiles)]
            terms = jnp.dot(weight, kernels[at], preferred_element_type=jnp.float32)
            results.append((control, terms[:ROWS] + terms[ROWS:]))
            squared = jnp.maximum(squares[at], 1e-12)
            radius = squared * lax.rsqrt(squared)
            inside = jnp.maximum(4.0 - radius, 0.0)
            inside = inside * inside
            kernel = inside * inside * (radius + 1.0)
            high = kernel.astype(jnp.bfloat16)
            kernels[at, :VT] = high
            kernels[at, VT:] = (kernel - high.astype(jnp.float32)).astype(jnp.bfloat16)
            _, volume, control = tiles_of(step_id * UNROLL + at)
            squares[at] = jnp.dot(
                nodes[volume], points[control], preferred_element_type=jnp.float32
            )
        for control, terms in results:
            loads_ref[control] = loads_ref[control] + terms
        return carry

    lax.fori_loop(0, (count + UNROLL - 1) // UNROLL + 2, pairs_step, 0)
    own_ref[...] = loads_ref[:tpb] * (1.0 / 256.0)
    spill_ref[...] = loads_ref[tpb:tiles] * (1.0 / 256.0)
    far_ref[...] = loads_ref[tiles:] * (1.0 / 256.0)
    for copy in copies:
        copy.wait()


def vmem(shape=None):
    return pl.BlockSpec(memory_space=pltpu.VMEM)


def smem():
    return pl.BlockSpec(memory_space=pltpu.SMEM)


def anywhere():
    return pl.BlockSpec(memory_space=pltpu.HBM)


def pair_stage(geometry, held_count, near_shape, pair_list, pair_count, place, sens, vol, ctl, inverse):
    ctiles, tpb, tiles = geometry
    vtiles = vol.shape[1] // VT
    columns = inverse.shape[1]
    out_shape = [
        jax.ShapeDtypeStruct((count, ROWS, CT), jnp.float32) for count in (tpb, tiles - tpb, 1)
    ]
    out_specs = [vmem()] * 3
    scratch = [
        pltpu.VMEM((vtiles, VT, DEPTH), jnp.bfloat16),
        pltpu.VMEM((tiles + 1, DEPTH, CT), jnp.bfloat16),
        pltpu.VMEM((vtiles + 1, 2 * ROWS, 2 * VT), jnp.bfloat16),
        pltpu.VMEM((tiles + 1, ROWS, CT), jnp.float32),
        pltpu.VMEM((UNROLL, VT, CT), jnp.float32),
        pltpu.VMEM((UNROLL, 2 * VT, CT), jnp.bfloat16),
        pltpu.VMEM(sens.shape, jnp.float32),
        pltpu.VMEM(vol.shape, jnp.float32),
        pltpu.VMEM(ctl.shape, jnp.float32),
        pltpu.SMEM(pair_list.shape, jnp.int32),
        pltpu.SemaphoreType.DMA((4,)),
    ]
    if held_count:
        out_shape += [pltpu.VMEM((PIECE, columns), inverse.dtype)] * held_count
        out_specs += [vmem()] * held_count
        pieces, depth, width = near_shape
        out_shape.append(pltpu.VMEM((depth, pieces * width), inverse.dtype))
        out_specs.append(vmem())
        scratch.append(pltpu.SemaphoreType.DMA((held_count + pieces,)))
    return pl.pallas_call(
        functools.partial(pair_kernel, geometry, held_count, 1 if held_count else 0),
        out_shape=out_shape,
        in_specs=[smem(), smem()] + [anywhere()] * 5,
        out_specs=out_specs,
        scratch_shapes=scratch,
        compiler_params=pltpu.CompilerParams(vmem_limit_bytes=10 * MIB),
        cost_estimate=pl.CostEstimate(
            flops=512 * 16384 * 400, bytes_accessed=held_count * PIECE * columns * 2, transcendentals=0
        ),
        name="pairs",
    )(
        pair_count,
        place,
        *[pltpu.with_memory_space_constraint(x, pltpu.HBM) for x in (pair_list, sens, vol, ctl)],
        inverse,
    )


def held_part(row_loads, held_refs, columns):
    value = jnp.zeros((2 * ROWS, columns.size), jnp.float32)
    for piece, held_ref in enumerate(held_refs):
        value = value + jnp.dot(
            row_loads[:, piece * PIECE : (piece + 1) * PIECE],
            held_ref[:, columns],
            preferred_element_type=jnp.float32,
        )
    return value[:ROWS]


def multiply(orders, me, row_loads, held_refs, inverse_ref, out_refs, partial, ring, sems):
    slots, streamed, chunk = ring.shape
    held = inverse_ref.shape[0] - streamed
    count = len(orders)
    per_out = count // len(out_refs)

    def columns_of(at):
        return pl.ds(chunk_start(me, *orders[at], chunk), chunk)

    def fetch(at):
        return pltpu.make_async_copy(
            inverse_ref.at[pl.ds(held, streamed), columns_of(at)],
            ring.at[at % slots],
            sems.at[at % slots],
        )

    for at in range(slots):
        fetch(at).start()
    yield
    for at in range(AHEAD):
        partial[at] = held_part(row_loads, held_refs, columns_of(at))
    for at in range(count):
        if at + AHEAD < count:
            partial[(at + AHEAD) % (AHEAD + 1)] = held_part(
                row_loads, held_refs, columns_of(at + AHEAD)
            )
        fetch(at).wait()
        value = jnp.dot(
            row_loads[:, held:], ring[at % slots], preferred_element_type=jnp.float32
        )
        if at + slots < count:
            fetch(at + slots).start()
        out_ref = out_refs[at // per_out]
        place = at % per_out
        out_ref[:, place * chunk : (place + 1) * chunk] = (
            partial[at % (AHEAD + 1)] + value[:ROWS]
        ).astype(out_ref.dtype)
    yield


def first_kernel(
    orders,
    offsets,
    place_ref,
    own_ref,
    partner_ref,
    spill_a_ref,
    spill_b_ref,
    far_same_ref,
    far_cross_ref,
    *rest,
):
    held_refs = rest[:-9]
    _, inverse_ref, row_loads, *out_refs, partial, ring, sems = rest[-9:]
    tpb = partner_ref.shape[0]
    spilled = spill_a_ref.shape[0]
    even = place_ref[3] == 0
    steps = multiply(
        orders,
        place_ref[2],
        row_loads,
        held_refs,
        inverse_ref,
        out_refs,
        partial,
        ring,
        sems,
    )
    next(steps)
    for tile in range(tpb):
        total = own_ref[tile] + partner_ref[tile]
        if tile < spilled:
            total = total + jnp.where(even, spill_a_ref[tile], spill_b_ref[tile])
        if tile == offsets[0]:
            total = total + jnp.where(even, far_same_ref[0], far_cross_ref[0])
        if tile == offsets[1]:
            total = total + jnp.where(even, far_cross_ref[0], far_same_ref[0])
        both = jnp.concatenate([total, jnp.zeros_like(total)], axis=0)
        row_loads[:, tile * CT : (tile + 1) * CT] = both.astype(jnp.bfloat16)
    next(steps)


def near_kernel(count, place_ref, row_loads, *rest):
    *held_refs, near_ref, out_ref = rest
    held = len(held_refs) * PIECE
    chunk = near_ref.shape[1] // count
    for at in range(count):
        place = slice(at * chunk, (at + 1) * chunk)
        columns = pl.ds(chunk_start(place_ref[2], 0, at, chunk), chunk)
        value = held_part(row_loads, held_refs, columns)
        value = value + jnp.dot(
            row_loads[:, held:], near_ref[:, place], preferred_element_type=jnp.float32
        )[:ROWS]
        out_ref[:, place] = value


def product_stage(kernel, small, pinned, rest, outs, scratch, name):
    return pl.pallas_call(
        kernel,
        out_shape=outs,
        in_specs=[smem()] + [vmem()] * (len(small) - 1 + len(pinned)) + [anywhere()] * len(rest),
        out_specs=[vmem()] * len(outs),
        scratch_shapes=scratch,
        compiler_params=pltpu.CompilerParams(vmem_limit_bytes=PRODUCT_MIB * MIB),
        cost_estimate=pl.CostEstimate(
            flops=16 * 2048 * 4096, bytes_accessed=16 * MIB, transcendentals=0
        ),
        name=name,
    )(*small, *[pltpu.with_memory_space_constraint(piece, pltpu.VMEM) for piece in pinned], *rest)


def local(wide, narrow, sensitivity, vol_coord, ctl_coord, pair_list, pair_count, inverse):
    devices = wide * narrow
    components = sensitivity.shape[0]
    ctiles = ctl_coord.shape[1] // CT
    row_count, columns = inverse.shape
    tpb = row_count // CT
    offsets = [
        max((w * narrow + n) * ctiles // devices - w * tpb for w in range(wide))
        for n in range(narrow)
    ]
    tiles = max(offsets) + BAND
    w = lax.axis_index("wide")
    n = lax.axis_index("narrow")
    me = w * narrow + n
    far_tile = (me + devices // 2) % devices * ctiles // devices
    place = jnp.stack([w * tpb, far_tile, w, n]).astype(jnp.int32)
    geometry = (ctiles, tpb, tiles)

    chunk = columns // wide
    fast = (
        narrow == 2
        and wide >= 8
        and wide & (wide - 1) == 0
        and chunk % CT == 0
        and tiles <= 2 * tpb
        and max(offsets[0] + BAND, 0) <= tpb
        and row_count == 8 * PIECE
    )
    if not fast:
        own, spill, far_tile_loads = pair_stage(
            geometry, 0, (), pair_list, pair_count, place, sensitivity, vol_coord, ctl_coord, inverse
        )
        spans = -(-tiles // tpb)
        band = jnp.pad(spill, ((0, spans * tpb - tiles), (0, 0), (0, 0)))
        block = own
        for shift in range(1, spans):
            part = band[(shift - 1) * tpb : shift * tpb]
            block = block + lax.ppermute(
                part, "wide", [(at, (at + shift) % wide) for at in range(wide)]
            )
        far_row = far_tile % tpb
        far = jnp.zeros((tpb, ROWS, CT), jnp.float32)
        far = lax.dynamic_update_slice(far, far_tile_loads, (far_row, 0, 0))
        far_shift = wide // 2
        block = block + lax.ppermute(
            far, "wide", [(at, (at + far_shift) % wide) for at in range(wide)]
        )
        block = lax.psum(block, "narrow")
        row_loads = block.transpose(1, 0, 2).reshape(ROWS, row_count)[:components]
        terms = jnp.dot(
            row_loads.astype(jnp.bfloat16), inverse, preferred_element_type=jnp.float32
        )
        return lax.psum_scatter(terms, "wide", scatter_dimension=1, tiled=True)

    ends = range(wide // 4)
    streamed = row_count - HELD * PIECE
    own, spill, far, *pinned = pair_stage(
        geometry,
        HELD,
        (len(ends), streamed, chunk),
        pair_list,
        pair_count,
        place,
        sensitivity,
        vol_coord,
        ctl_coord,
        inverse,
    )
    held, near = pinned[:HELD], pinned[HELD:]
    both = ("wide", "narrow")
    partner = lax.ppermute(own, "narrow", [(0, 1), (1, 0)])

    def index(at_w, at_n):
        return (at_w % wide) * narrow + at_n

    spans = range(wide)
    half = wide // 2
    straight = [lambda at, k=k: (at, (at + k) % wide) for k in (1, half)]
    cross = [
        [(index(at, k), index(at + shift, 1 - k)) for at in spans for k in range(2)]
        for shift in (1, half)
    ]
    spill_b = lax.ppermute(spill, "wide", [straight[0](at) for at in spans])
    spill_a = lax.ppermute(spill, both, cross[0])
    far_same = lax.ppermute(far, "wide", [straight[1](at) for at in spans])
    far_cross = lax.ppermute(far, both, cross[1])
    quarter = columns // 4
    orders = [(difference, end) for difference in (3, 2, 1) for end in ends]
    parts = product_stage(
        functools.partial(first_kernel, orders, offsets),
        [place, own, partner, spill_a, spill_b, far_same, far_cross],
        held + near,
        [inverse],
        [
            pltpu.VMEM((2 * ROWS, row_count), jnp.bfloat16),
            jax.ShapeDtypeStruct((ROWS, quarter), jnp.bfloat16),
            jax.ShapeDtypeStruct((ROWS, quarter), jnp.bfloat16),
            jax.ShapeDtypeStruct((ROWS, quarter), jnp.float32),
        ],
        [
            pltpu.VMEM((AHEAD + 1, ROWS, chunk), jnp.float32),
            pltpu.VMEM((SLOTS, streamed, chunk), inverse.dtype),
            pltpu.SemaphoreType.DMA((SLOTS,)),
        ],
        "product_a",
    )
    row_loads = parts[0]
    moved = [
        lax.ppermute(part, "wide", [(at, at ^ difference) for at in spans])
        for part, difference in zip(parts[1:], (3, 2, 1))
    ]
    (total,) = product_stage(
        functools.partial(near_kernel, len(ends)),
        [place, row_loads],
        held + near,
        [],
        [jax.ShapeDtypeStruct((ROWS, quarter), jnp.float32)],
        [],
        "product_b",
    )
    for part in moved:
        total = total + part.astype(jnp.float32)
    result = total[:, :chunk]
    for end in ends[1:]:
        sent = total[:, end * chunk : (end + 1) * chunk].astype(jnp.bfloat16)
        got = lax.ppermute(sent, "wide", [(at, at ^ (end << 2)) for at in spans])
        result = result + got.astype(jnp.float32)
    return result[:components]


def solution(mesh):
    return jax.shard_map(
        functools.partial(local, mesh.shape["wide"], mesh.shape["narrow"]),
        mesh=mesh,
        in_specs=(
            P(None, ("wide", "narrow")),
            P(None, ("wide", "narrow")),
            P(),
            P(None, ("wide", "narrow")),
            P(("wide", "narrow")),
            P("wide", "narrow"),
        ),
        out_specs=P(None, ("narrow", "wide")),
        check_vma=False,
    )
```

```python
import functools

import jax
import jax.numpy as jnp
from jax import lax
from jax.experimental import pallas as pl
from jax.experimental.pallas import tpu as pltpu
from jax.sharding import PartitionSpec as P

CT = 128
VT = 128
BAND = 16
UNROLL = 8
AHEAD = 2
ROWS = 8
DEPTH = 64
MIB = 1 << 20
PIECE = 256
HELD = 4
SLOTS = 3
PRODUCT_MIB = 7


def thirds(value):
    high = value.astype(jnp.bfloat16).astype(jnp.float32)
    rest = value - high
    middle = rest.astype(jnp.bfloat16).astype(jnp.float32)
    return high, middle, rest - middle


def features(coords, is_node):
    width = coords.shape[1]
    scaled = 4.0 * coords - 2.0
    norm = scaled[0:1] * scaled[0:1] + scaled[1:2] * scaled[1:2] + scaled[2:3] * scaled[2:3]
    padded = jnp.concatenate([scaled, jnp.zeros((ROWS - 3, width), jnp.float32)], axis=0)
    high, middle, low = thirds(padded)
    row = lax.broadcasted_iota(jnp.int32, (ROWS, width), 0)
    n_high, n_middle, n_low = thirds(jnp.broadcast_to(norm, (ROWS, width)))
    first = 0 if is_node else 3
    norms = jnp.where(
        row == first,
        n_high,
        jnp.where(row == first + 1, n_middle, jnp.where(row == first + 2, n_low, 0.0)),
    )
    ones = jnp.where((row >= 3 - first) & (row < 6 - first), 1.0, 0.0)
    last = norms + ones
    if is_node:
        parts = [high, high, middle, middle, high, low, last]
    else:
        parts = [high, middle, high, middle, low, high]
        parts = [-2.0 * part for part in parts] + [last]
    parts = parts + [jnp.zeros((DEPTH - ROWS * len(parts), width), jnp.float32)]
    return jnp.concatenate(parts, axis=0)


def chunk_start(me, near, far, chunk):
    return pl.multiple_of(((far << 2) + ((me & 3) ^ near)) * chunk, chunk)


def held_copies(me, inverse_ref, held_refs, near_refs, sems=None):
    copies = []
    for at, held_ref in enumerate(held_refs):
        rows = pl.ds(at * PIECE, PIECE)
        copies.append(pltpu.make_async_copy(inverse_ref.at[rows, :], held_ref, sems.at[at]))
    for near_ref in near_refs:
        depth, width = near_ref.shape
        rows = pl.ds(len(held_refs) * PIECE, depth)
        pieces = sems.shape[0] - len(held_refs)
        chunk = width // pieces
        for at in range(pieces):
            columns = pl.ds(chunk_start(me, 0, at, chunk), chunk)
            copies.append(
                pltpu.make_async_copy(
                    inverse_ref.at[rows, columns],
                    near_ref.at[:, pl.ds(at * chunk, chunk)],
                    sems.at[len(held_refs) + at],
                )
            )
    return copies


def pair_kernel(
    geometry,
    held_count,
    near_count,
    count_ref,
    place_ref,
    listed_ref,
    sens_ref,
    vol_ref,
    ctl_ref,
    inverse_ref,
    own_ref,
    spill_ref,
    far_ref,
    *rest,
):
    ctiles, tpb, tiles = geometry
    held_refs, rest = rest[:held_count], rest[held_count:]
    near_refs, rest = rest[:near_count], rest[near_count:]
    nodes, points, weights, loads_ref, squares, kernels, sens_in, vol_in, ctl_in, list_ref, in_sems = (
        rest[:11]
    )
    vtiles = vol_ref.shape[1] // VT
    slots = list_ref.shape[1]
    inputs = [
        pltpu.make_async_copy(source, target, in_sems.at[at])
        for at, (source, target) in enumerate(
            [
                (vol_ref, vol_in),
                (ctl_ref, ctl_in),
                (sens_ref, sens_in),
                (listed_ref, list_ref),
            ]
        )
    ]
    for copy in inputs:
        copy.start()
    copies = held_copies(place_ref[2], inverse_ref, held_refs, near_refs, *rest[11:])

    first_tile = place_ref[0]
    far_tile = place_ref[1]

    loads_ref[...] = jnp.zeros(loads_ref.shape, jnp.float32)
    squares[...] = jnp.zeros(squares.shape, jnp.float32)
    kernels[...] = jnp.zeros(kernels.shape, jnp.bfloat16)
    weights[vtiles] = jnp.zeros(weights.shape[1:], jnp.bfloat16)
    for copy in inputs:
        copy.wait()
    for copy in copies:
        copy.start()

    group = 8
    square = (VT, VT)
    same = lax.broadcasted_iota(jnp.int32, square, 0) == lax.broadcasted_iota(jnp.int32, square, 1)
    unit = jnp.where(same, 1.0, 0.0).astype(jnp.bfloat16)

    def node_group(group_id, carry):
        begin = pl.multiple_of(group_id * (group * VT), group * VT)
        rows = features(vol_in[:, pl.ds(begin, group * VT)], True).astype(jnp.bfloat16)
        sens = sens_in[:, pl.ds(begin, group * VT)]
        components = sens.shape[0]
        if components < ROWS:
            sens = jnp.concatenate(
                [sens, jnp.zeros((ROWS - components, group * VT), jnp.float32)], axis=0
            )
        high = sens.astype(jnp.bfloat16).astype(jnp.float32)
        both = jnp.concatenate([high, sens - high], axis=0).astype(jnp.bfloat16)
        for at in range(group):
            cut = slice(at * VT, (at + 1) * VT)
            turned = lax.dot_general(
                unit, rows[:, cut], (((1,), (1,)), ((), ())), preferred_element_type=jnp.float32
            )
            nodes[group_id * group + at] = turned.astype(jnp.bfloat16)
            weights[group_id * group + at] = jnp.concatenate([both[:, cut], both[:, cut]], axis=1)
        return carry

    lax.fori_loop(0, vtiles // group, node_group, 0)

    for tile in range(tiles + 1):
        named = lax.rem(first_tile + tile, ctiles) if tile < tiles else far_tile
        begin = pl.multiple_of(named * CT, CT)
        points[tile] = features(ctl_in[:, pl.ds(begin, CT)], False).astype(jnp.bfloat16)

    count = count_ref[0]

    def tiles_of(slot):
        live = (slot >= 0) & (slot < count)
        at = jnp.minimum(jnp.maximum(slot, 0), slots - 1)
        volume = jnp.where(live, list_ref[0, at], 0)
        control = list_ref[1, at] - first_tile
        control = jnp.where(control < 0, control + ctiles, control)
        control = jnp.where(slot == 0, tiles, control)
        control = jnp.where(live, control, 0)
        return live, volume, control

    def pairs_step(step_id, carry):
        results = []
        for at in range(UNROLL):
            if at % 2 == 0:
                controls, pair_weights = [], []
                for slot in ((step_id - 2) * UNROLL + at, (step_id - 2) * UNROLL + at + 1):
                    live, volume, control = tiles_of(slot)
                    pair_weights.append(weights[jnp.where(live, volume, vtiles)])
                    controls.append(control)
                terms = jnp.dot(
                    jnp.concatenate(pair_weights, axis=0),
                    kernels[at // 2],
                    preferred_element_type=jnp.float32,
                )
                results.append((controls[0], terms[:ROWS, :CT] + terms[ROWS : 2 * ROWS, :CT]))
                results.append((controls[1], terms[2 * ROWS : 3 * ROWS, CT:] + terms[3 * ROWS :, CT:]))
            squared = jnp.maximum(squares[at], 1e-12)
            radius = squared * lax.rsqrt(squared)
            inside = jnp.maximum(4.0 - radius, 0.0)
            inside = inside * inside
            kernel = inside * inside * (radius + 1.0)
            high = kernel.astype(jnp.bfloat16)
            place = slice((at % 2) * CT, (at % 2 + 1) * CT)
            kernels[at // 2, :VT, place] = high
            kernels[at // 2, VT:, place] = (kernel - high.astype(jnp.float32)).astype(jnp.bfloat16)
            _, volume, control = tiles_of(step_id * UNROLL + at)
            squares[at] = jnp.dot(
                nodes[volume], points[control], preferred_element_type=jnp.float32
            )
        for control, terms in results:
            loads_ref[control] = loads_ref[control] + terms
        return carry

    lax.fori_loop(0, (count + UNROLL - 1) // UNROLL + 2, pairs_step, 0)
    own_ref[...] = loads_ref[:tpb] * (1.0 / 256.0)
    spill_ref[...] = loads_ref[tpb:tiles] * (1.0 / 256.0)
    far_ref[...] = loads_ref[tiles:] * (1.0 / 256.0)
    for copy in copies:
        copy.wait()


def vmem(shape=None):
    return pl.BlockSpec(memory_space=pltpu.VMEM)


def smem():
    return pl.BlockSpec(memory_space=pltpu.SMEM)


def anywhere():
    return pl.BlockSpec(memory_space=pltpu.HBM)


def pair_stage(geometry, held_count, near_shape, pair_list, pair_count, place, sens, vol, ctl, inverse):
    ctiles, tpb, tiles = geometry
    vtiles = vol.shape[1] // VT
    columns = inverse.shape[1]
    out_shape = [
        jax.ShapeDtypeStruct((count, ROWS, CT), jnp.float32) for count in (tpb, tiles - tpb, 1)
    ]
    out_specs = [vmem()] * 3
    scratch = [
        pltpu.VMEM((vtiles, VT, DEPTH), jnp.bfloat16),
        pltpu.VMEM((tiles + 1, DEPTH, CT), jnp.bfloat16),
        pltpu.VMEM((vtiles + 1, 2 * ROWS, 2 * VT), jnp.bfloat16),
        pltpu.VMEM((tiles + 1, ROWS, CT), jnp.float32),
        pltpu.VMEM((UNROLL, VT, CT), jnp.float32),
        pltpu.VMEM((UNROLL // 2, 2 * VT, 2 * CT), jnp.bfloat16),
        pltpu.VMEM(sens.shape, jnp.float32),
        pltpu.VMEM(vol.shape, jnp.float32),
        pltpu.VMEM(ctl.shape, jnp.float32),
        pltpu.SMEM(pair_list.shape, jnp.int32),
        pltpu.SemaphoreType.DMA((4,)),
    ]
    if held_count:
        out_shape += [pltpu.VMEM((PIECE, columns), inverse.dtype)] * held_count
        out_specs += [vmem()] * held_count
        pieces, depth, width = near_shape
        out_shape.append(pltpu.VMEM((depth, pieces * width), inverse.dtype))
        out_specs.append(vmem())
        scratch.append(pltpu.SemaphoreType.DMA((held_count + pieces,)))
    return pl.pallas_call(
        functools.partial(pair_kernel, geometry, held_count, 1 if held_count else 0),
        out_shape=out_shape,
        in_specs=[smem(), smem()] + [anywhere()] * 5,
        out_specs=out_specs,
        scratch_shapes=scratch,
        compiler_params=pltpu.CompilerParams(vmem_limit_bytes=10 * MIB),
        cost_estimate=pl.CostEstimate(
            flops=512 * 16384 * 400, bytes_accessed=held_count * PIECE * columns * 2, transcendentals=0
        ),
        name="pairs",
    )(
        pair_count,
        place,
        *[pltpu.with_memory_space_constraint(x, pltpu.HBM) for x in (pair_list, sens, vol, ctl)],
        inverse,
    )


def held_part(row_loads, held_refs, columns):
    value = jnp.zeros((2 * ROWS, columns.size), jnp.float32)
    for piece, held_ref in enumerate(held_refs):
        value = value + jnp.dot(
            row_loads[:, piece * PIECE : (piece + 1) * PIECE],
            held_ref[:, columns],
            preferred_element_type=jnp.float32,
        )
    return value[:ROWS]


def multiply(orders, me, row_loads, held_refs, inverse_ref, out_refs, partial, ring, sems):
    slots, streamed, chunk = ring.shape
    held = inverse_ref.shape[0] - streamed
    count = len(orders)
    per_out = count // len(out_refs)

    def columns_of(at):
        return pl.ds(chunk_start(me, *orders[at], chunk), chunk)

    def fetch(at):
        return pltpu.make_async_copy(
            inverse_ref.at[pl.ds(held, streamed), columns_of(at)],
            ring.at[at % slots],
            sems.at[at % slots],
        )

    for at in range(slots):
        fetch(at).start()
    yield
    for at in range(AHEAD):
        partial[at] = held_part(row_loads, held_refs, columns_of(at))
    for at in range(count):
        if at + AHEAD < count:
            partial[(at + AHEAD) % (AHEAD + 1)] = held_part(
                row_loads, held_refs, columns_of(at + AHEAD)
            )
        fetch(at).wait()
        value = jnp.dot(
            row_loads[:, held:], ring[at % slots], preferred_element_type=jnp.float32
        )
        if at + slots < count:
            fetch(at + slots).start()
        out_ref = out_refs[at // per_out]
        place = at % per_out
        out_ref[:, place * chunk : (place + 1) * chunk] = (
            partial[at % (AHEAD + 1)] + value[:ROWS]
        ).astype(out_ref.dtype)
    yield


def first_kernel(
    orders,
    offsets,
    place_ref,
    own_ref,
    partner_ref,
    spill_a_ref,
    spill_b_ref,
    far_same_ref,
    far_cross_ref,
    *rest,
):
    held_refs = rest[:-9]
    _, inverse_ref, row_loads, *out_refs, partial, ring, sems = rest[-9:]
    tpb = partner_ref.shape[0]
    spilled = spill_a_ref.shape[0]
    even = place_ref[3] == 0
    steps = multiply(
        orders,
        place_ref[2],
        row_loads,
        held_refs,
        inverse_ref,
        out_refs,
        partial,
        ring,
        sems,
    )
    next(steps)
    for tile in range(tpb):
        total = own_ref[tile] + partner_ref[tile]
        if tile < spilled:
            total = total + jnp.where(even, spill_a_ref[tile], spill_b_ref[tile])
        if tile == offsets[0]:
            total = total + jnp.where(even, far_same_ref[0], far_cross_ref[0])
        if tile == offsets[1]:
            total = total + jnp.where(even, far_cross_ref[0], far_same_ref[0])
        both = jnp.concatenate([total, jnp.zeros_like(total)], axis=0)
        row_loads[:, tile * CT : (tile + 1) * CT] = both.astype(jnp.bfloat16)
    next(steps)


def near_kernel(count, place_ref, row_loads, *rest):
    *held_refs, near_ref, out_ref = rest
    held = len(held_refs) * PIECE
    chunk = near_ref.shape[1] // count
    for at in range(count):
        place = slice(at * chunk, (at + 1) * chunk)
        columns = pl.ds(chunk_start(place_ref[2], 0, at, chunk), chunk)
        value = held_part(row_loads, held_refs, columns)
        value = value + jnp.dot(
            row_loads[:, held:], near_ref[:, place], preferred_element_type=jnp.float32
        )[:ROWS]
        out_ref[:, place] = value


def product_stage(kernel, small, pinned, rest, outs, scratch, name):
    return pl.pallas_call(
        kernel,
        out_shape=outs,
        in_specs=[smem()] + [vmem()] * (len(small) - 1 + len(pinned)) + [anywhere()] * len(rest),
        out_specs=[vmem()] * len(outs),
        scratch_shapes=scratch,
        compiler_params=pltpu.CompilerParams(vmem_limit_bytes=PRODUCT_MIB * MIB),
        cost_estimate=pl.CostEstimate(
            flops=16 * 2048 * 4096, bytes_accessed=16 * MIB, transcendentals=0
        ),
        name=name,
    )(*small, *[pltpu.with_memory_space_constraint(piece, pltpu.VMEM) for piece in pinned], *rest)


def local(wide, narrow, sensitivity, vol_coord, ctl_coord, pair_list, pair_count, inverse):
    devices = wide * narrow
    components = sensitivity.shape[0]
    ctiles = ctl_coord.shape[1] // CT
    row_count, columns = inverse.shape
    tpb = row_count // CT
    offsets = [
        max((w * narrow + n) * ctiles // devices - w * tpb for w in range(wide))
        for n in range(narrow)
    ]
    tiles = max(offsets) + BAND
    w = lax.axis_index("wide")
    n = lax.axis_index("narrow")
    me = w * narrow + n
    far_tile = (me + devices // 2) % devices * ctiles // devices
    place = jnp.stack([w * tpb, far_tile, w, n]).astype(jnp.int32)
    geometry = (ctiles, tpb, tiles)

    chunk = columns // wide
    fast = (
        narrow == 2
        and wide >= 8
        and wide & (wide - 1) == 0
        and chunk % CT == 0
        and tiles <= 2 * tpb
        and max(offsets[0] + BAND, 0) <= tpb
        and row_count == 8 * PIECE
    )
    if not fast:
        own, spill, far_tile_loads = pair_stage(
            geometry, 0, (), pair_list, pair_count, place, sensitivity, vol_coord, ctl_coord, inverse
        )
        spans = -(-tiles // tpb)
        band = jnp.pad(spill, ((0, spans * tpb - tiles), (0, 0), (0, 0)))
        block = own
        for shift in range(1, spans):
            part = band[(shift - 1) * tpb : shift * tpb]
            block = block + lax.ppermute(
                part, "wide", [(at, (at + shift) % wide) for at in range(wide)]
            )
        far_row = far_tile % tpb
        far = jnp.zeros((tpb, ROWS, CT), jnp.float32)
        far = lax.dynamic_update_slice(far, far_tile_loads, (far_row, 0, 0))
        far_shift = wide // 2
        block = block + lax.ppermute(
            far, "wide", [(at, (at + far_shift) % wide) for at in range(wide)]
        )
        block = lax.psum(block, "narrow")
        row_loads = block.transpose(1, 0, 2).reshape(ROWS, row_count)[:components]
        terms = jnp.dot(
            row_loads.astype(jnp.bfloat16), inverse, preferred_element_type=jnp.float32
        )
        return lax.psum_scatter(terms, "wide", scatter_dimension=1, tiled=True)

    ends = range(wide // 4)
    streamed = row_count - HELD * PIECE
    own, spill, far, *pinned = pair_stage(
        geometry,
        HELD,
        (len(ends), streamed, chunk),
        pair_list,
        pair_count,
        place,
        sensitivity,
        vol_coord,
        ctl_coord,
        inverse,
    )
    held, near = pinned[:HELD], pinned[HELD:]
    both = ("wide", "narrow")
    partner = lax.ppermute(own, "narrow", [(0, 1), (1, 0)])

    def index(at_w, at_n):
        return (at_w % wide) * narrow + at_n

    spans = range(wide)
    half = wide // 2
    straight = [lambda at, k=k: (at, (at + k) % wide) for k in (1, half)]
    cross = [
        [(index(at, k), index(at + shift, 1 - k)) for at in spans for k in range(2)]
        for shift in (1, half)
    ]
    spill_b = lax.ppermute(spill, "wide", [straight[0](at) for at in spans])
    spill_a = lax.ppermute(spill, both, cross[0])
    far_same = lax.ppermute(far, "wide", [straight[1](at) for at in spans])
    far_cross = lax.ppermute(far, both, cross[1])
    quarter = columns // 4
    orders = [(difference, end) for difference in (3, 2, 1) for end in ends]
    parts = product_stage(
        functools.partial(first_kernel, orders, offsets),
        [place, own, partner, spill_a, spill_b, far_same, far_cross],
        held + near,
        [inverse],
        [
            pltpu.VMEM((2 * ROWS, row_count), jnp.bfloat16),
            jax.ShapeDtypeStruct((ROWS, quarter), jnp.bfloat16),
            jax.ShapeDtypeStruct((ROWS, quarter), jnp.bfloat16),
            jax.ShapeDtypeStruct((ROWS, quarter), jnp.float32),
        ],
        [
            pltpu.VMEM((AHEAD + 1, ROWS, chunk), jnp.float32),
            pltpu.VMEM((SLOTS, streamed, chunk), inverse.dtype),
            pltpu.SemaphoreType.DMA((SLOTS,)),
        ],
        "product_a",
    )
    row_loads = parts[0]
    moved = [
        lax.ppermute(part, "wide", [(at, at ^ difference) for at in spans])
        for part, difference in zip(parts[1:], (3, 2, 1))
    ]
    (total,) = product_stage(
        functools.partial(near_kernel, len(ends)),
        [place, row_loads],
        held + near,
        [],
        [jax.ShapeDtypeStruct((ROWS, quarter), jnp.float32)],
        [],
        "product_b",
    )
    for part in moved:
        total = total + part.astype(jnp.float32)
    total = total.reshape(ROWS, len(ends), chunk).transpose(1, 0, 2)
    sent = total.astype(jnp.bfloat16)
    groups = [[(end << 2) + low for end in ends] for low in range(4)]
    got = lax.all_to_all(sent, "wide", 0, 0, axis_index_groups=groups, tiled=True)
    return jnp.sum(got.astype(jnp.float32), axis=0)[:components]


def solution(mesh):
    return jax.shard_map(
        functools.partial(local, mesh.shape["wide"], mesh.shape["narrow"]),
        mesh=mesh,
        in_specs=(
            P(None, ("wide", "narrow")),
            P(None, ("wide", "narrow")),
            P(),
            P(None, ("wide", "narrow")),
            P(("wide", "narrow")),
            P("wide", "narrow"),
        ),
        out_specs=P(None, ("narrow", "wide")),
        check_vma=False,
    )
```

```python
import functools

import jax
import jax.numpy as jnp
from jax import lax
from jax.experimental import pallas as pl
from jax.experimental.pallas import tpu as pltpu
from jax.sharding import PartitionSpec as P

CT = 128
VT = 128
BAND = 16
UNROLL = 8
AHEAD = 4
ROWS = 8
DEPTH = 64
MIB = 1 << 20
PIECE = 256
HELD = 4
SLOTS = 4
PRODUCT_MIB = 9


def thirds(value):
    high = value.astype(jnp.bfloat16).astype(jnp.float32)
    rest = value - high
    middle = rest.astype(jnp.bfloat16).astype(jnp.float32)
    return high, middle, rest - middle


def features(coords, is_node):
    width = coords.shape[1]
    scaled = 4.0 * coords - 2.0
    norm = scaled[0:1] * scaled[0:1] + scaled[1:2] * scaled[1:2] + scaled[2:3] * scaled[2:3]
    padded = jnp.concatenate([scaled, jnp.zeros((ROWS - 3, width), jnp.float32)], axis=0)
    high, middle, low = thirds(padded)
    row = lax.broadcasted_iota(jnp.int32, (ROWS, width), 0)
    n_high, n_middle, n_low = thirds(jnp.broadcast_to(norm, (ROWS, width)))
    first = 0 if is_node else 3
    norms = jnp.where(
        row == first,
        n_high,
        jnp.where(row == first + 1, n_middle, jnp.where(row == first + 2, n_low, 0.0)),
    )
    ones = jnp.where((row >= 3 - first) & (row < 6 - first), 1.0, 0.0)
    last = norms + ones
    if is_node:
        parts = [high, high, middle, middle, high, low, last]
    else:
        parts = [high, middle, high, middle, low, high]
        parts = [-2.0 * part for part in parts] + [last]
    parts = parts + [jnp.zeros((DEPTH - ROWS * len(parts), width), jnp.float32)]
    return jnp.concatenate(parts, axis=0)


def chunk_start(me, near, far, chunk):
    return pl.multiple_of((me ^ (near | (far << 2))) * chunk, chunk)


def held_copies(me, inverse_ref, held_refs, near_refs, sems=None):
    copies = []
    for at, held_ref in enumerate(held_refs):
        rows = pl.ds(at * PIECE, PIECE)
        copies.append(pltpu.make_async_copy(inverse_ref.at[rows, :], held_ref, sems.at[at]))
    for near_ref in near_refs:
        depth, width = near_ref.shape
        rows = pl.ds(len(held_refs) * PIECE, depth)
        pieces = sems.shape[0] - len(held_refs)
        chunk = width // pieces
        for at in range(pieces):
            columns = pl.ds(chunk_start(me, 0, at, chunk), chunk)
            copies.append(
                pltpu.make_async_copy(
                    inverse_ref.at[rows, columns],
                    near_ref.at[:, pl.ds(at * chunk, chunk)],
                    sems.at[len(held_refs) + at],
                )
            )
    return copies


def pair_kernel(
    geometry,
    held_count,
    near_count,
    count_ref,
    place_ref,
    listed_ref,
    sens_ref,
    vol_ref,
    ctl_ref,
    inverse_ref,
    own_ref,
    spill_ref,
    far_ref,
    *rest,
):
    ctiles, tpb, tiles = geometry
    held_refs, rest = rest[:held_count], rest[held_count:]
    near_refs, rest = rest[:near_count], rest[near_count:]
    nodes, points, weights, loads_ref, squares, kernels, sens_in, vol_in, ctl_in, list_ref, in_sems = (
        rest[:11]
    )
    vtiles = vol_ref.shape[1] // VT
    slots = list_ref.shape[1]
    inputs = [
        pltpu.make_async_copy(source, target, in_sems.at[at])
        for at, (source, target) in enumerate(
            [
                (vol_ref, vol_in),
                (ctl_ref, ctl_in),
                (sens_ref, sens_in),
                (listed_ref, list_ref),
            ]
        )
    ]
    for copy in inputs:
        copy.start()
    copies = held_copies(place_ref[2], inverse_ref, held_refs, near_refs, *rest[11:])

    first_tile = place_ref[0]
    far_tile = place_ref[1]

    loads_ref[...] = jnp.zeros(loads_ref.shape, jnp.float32)
    squares[...] = jnp.zeros(squares.shape, jnp.float32)
    kernels[...] = jnp.zeros(kernels.shape, jnp.bfloat16)
    weights[vtiles] = jnp.zeros(weights.shape[1:], jnp.bfloat16)
    for copy in inputs:
        copy.wait()
    for copy in copies:
        copy.start()

    group = 8
    square = (VT, VT)
    same = lax.broadcasted_iota(jnp.int32, square, 0) == lax.broadcasted_iota(jnp.int32, square, 1)
    unit = jnp.where(same, 1.0, 0.0).astype(jnp.bfloat16)

    def node_group(group_id, carry):
        begin = pl.multiple_of(group_id * (group * VT), group * VT)
        rows = features(vol_in[:, pl.ds(begin, group * VT)], True).astype(jnp.bfloat16)
        sens = sens_in[:, pl.ds(begin, group * VT)]
        components = sens.shape[0]
        if components < ROWS:
            sens = jnp.concatenate(
                [sens, jnp.zeros((ROWS - components, group * VT), jnp.float32)], axis=0
            )
        high = sens.astype(jnp.bfloat16).astype(jnp.float32)
        both = jnp.concatenate([high, sens - high], axis=0).astype(jnp.bfloat16)
        for at in range(group):
            cut = slice(at * VT, (at + 1) * VT)
            turned = lax.dot_general(
                unit, rows[:, cut], (((1,), (1,)), ((), ())), preferred_element_type=jnp.float32
            )
            nodes[group_id * group + at] = turned.astype(jnp.bfloat16)
            weights[group_id * group + at] = jnp.concatenate([both[:, cut], both[:, cut]], axis=1)
        return carry

    lax.fori_loop(0, vtiles // group, node_group, 0)

    for tile in range(tiles + 1):
        named = lax.rem(first_tile + tile, ctiles) if tile < tiles else far_tile
        begin = pl.multiple_of(named * CT, CT)
        points[tile] = features(ctl_in[:, pl.ds(begin, CT)], False).astype(jnp.bfloat16)

    count = count_ref[0]

    def tiles_of(slot):
        live = (slot >= 0) & (slot < count)
        at = jnp.minimum(jnp.maximum(slot, 0), slots - 1)
        volume = jnp.where(live, list_ref[0, at], 0)
        control = list_ref[1, at] - first_tile
        control = jnp.where(control < 0, control + ctiles, control)
        control = jnp.where(slot == 0, tiles, control)
        control = jnp.where(live, control, 0)
        return live, volume, control

    def pairs_step(step_id, carry):
        results = []
        for at in range(UNROLL):
            if at % 2 == 0:
                controls, pair_weights = [], []
                for slot in ((step_id - 2) * UNROLL + at, (step_id - 2) * UNROLL + at + 1):
                    live, volume, control = tiles_of(slot)
                    pair_weights.append(weights[jnp.where(live, volume, vtiles)])
                    controls.append(control)
                terms = jnp.dot(
                    jnp.concatenate(pair_weights, axis=0),
                    kernels[at // 2],
                    preferred_element_type=jnp.float32,
                )
                results.append((controls[0], terms[:ROWS, :CT] + terms[ROWS : 2 * ROWS, :CT]))
                results.append((controls[1], terms[2 * ROWS : 3 * ROWS, CT:] + terms[3 * ROWS :, CT:]))
            squared = jnp.maximum(squares[at], 1e-12)
            radius = squared * lax.rsqrt(squared)
            inside = jnp.maximum(4.0 - radius, 0.0)
            inside = inside * inside
            kernel = inside * inside * (radius + 1.0)
            high = kernel.astype(jnp.bfloat16)
            place = slice((at % 2) * CT, (at % 2 + 1) * CT)
            kernels[at // 2, :VT, place] = high
            kernels[at // 2, VT:, place] = (kernel - high.astype(jnp.float32)).astype(jnp.bfloat16)
            _, volume, control = tiles_of(step_id * UNROLL + at)
            squares[at] = jnp.dot(
                nodes[volume], points[control], preferred_element_type=jnp.float32
            )
        for control, terms in results:
            loads_ref[control] = loads_ref[control] + terms
        return carry

    lax.fori_loop(0, (count + UNROLL - 1) // UNROLL + 2, pairs_step, 0)
    own_ref[...] = loads_ref[:tpb] * (1.0 / 256.0)
    spill_ref[...] = loads_ref[tpb:tiles] * (1.0 / 256.0)
    far_ref[...] = loads_ref[tiles:] * (1.0 / 256.0)
    for copy in copies:
        copy.wait()


def vmem(shape=None):
    return pl.BlockSpec(memory_space=pltpu.VMEM)


def smem():
    return pl.BlockSpec(memory_space=pltpu.SMEM)


def anywhere():
    return pl.BlockSpec(memory_space=pltpu.HBM)


def pair_stage(geometry, held_count, near_shape, pair_list, pair_count, place, sens, vol, ctl, inverse):
    ctiles, tpb, tiles = geometry
    vtiles = vol.shape[1] // VT
    columns = inverse.shape[1]
    out_shape = [
        jax.ShapeDtypeStruct((count, ROWS, CT), jnp.float32) for count in (tpb, tiles - tpb, 1)
    ]
    out_specs = [vmem()] * 3
    scratch = [
        pltpu.VMEM((vtiles, VT, DEPTH), jnp.bfloat16),
        pltpu.VMEM((tiles + 1, DEPTH, CT), jnp.bfloat16),
        pltpu.VMEM((vtiles + 1, 2 * ROWS, 2 * VT), jnp.bfloat16),
        pltpu.VMEM((tiles + 1, ROWS, CT), jnp.float32),
        pltpu.VMEM((UNROLL, VT, CT), jnp.float32),
        pltpu.VMEM((UNROLL // 2, 2 * VT, 2 * CT), jnp.bfloat16),
        pltpu.VMEM(sens.shape, jnp.float32),
        pltpu.VMEM(vol.shape, jnp.float32),
        pltpu.VMEM(ctl.shape, jnp.float32),
        pltpu.SMEM(pair_list.shape, jnp.int32),
        pltpu.SemaphoreType.DMA((4,)),
    ]
    if held_count:
        out_shape += [pltpu.VMEM((PIECE, columns), inverse.dtype)] * held_count
        out_specs += [vmem()] * held_count
        pieces, depth, width = near_shape
        out_shape.append(pltpu.VMEM((depth, pieces * width), inverse.dtype))
        out_specs.append(vmem())
        scratch.append(pltpu.SemaphoreType.DMA((held_count + pieces,)))
    return pl.pallas_call(
        functools.partial(pair_kernel, geometry, held_count, 1 if held_count else 0),
        out_shape=out_shape,
        in_specs=[smem(), smem()] + [anywhere()] * 5,
        out_specs=out_specs,
        scratch_shapes=scratch,
        compiler_params=pltpu.CompilerParams(vmem_limit_bytes=10 * MIB),
        cost_estimate=pl.CostEstimate(
            flops=512 * 16384 * 400, bytes_accessed=held_count * PIECE * columns * 2, transcendentals=0
        ),
        name="pairs",
    )(
        pair_count,
        place,
        *[pltpu.with_memory_space_constraint(x, pltpu.HBM) for x in (pair_list, sens, vol, ctl)],
        inverse,
    )


def held_part(row_loads, held_refs, columns):
    value = jnp.zeros((2 * ROWS, columns.size), jnp.float32)
    for piece, held_ref in enumerate(held_refs):
        value = value + jnp.dot(
            row_loads[:, piece * PIECE : (piece + 1) * PIECE],
            held_ref[:, columns],
            preferred_element_type=jnp.float32,
        )
    return value[:ROWS]


def multiply(orders, me, row_loads, held_refs, inverse_ref, out_refs, partial, ring, sems):
    slots, streamed, chunk = ring.shape
    held = inverse_ref.shape[0] - streamed
    count = len(orders)
    per_out = count // len(out_refs)

    def columns_of(at):
        return pl.ds(chunk_start(me, *orders[at], chunk), chunk)

    def fetch(at):
        return pltpu.make_async_copy(
            inverse_ref.at[pl.ds(held, streamed), columns_of(at)],
            ring.at[at % slots],
            sems.at[at % slots],
        )

    for at in range(slots):
        fetch(at).start()
    yield
    for at in range(AHEAD):
        partial[at] = held_part(row_loads, held_refs, columns_of(at))
    for at in range(count):
        if at + AHEAD < count:
            partial[(at + AHEAD) % (AHEAD + 1)] = held_part(
                row_loads, held_refs, columns_of(at + AHEAD)
            )
        fetch(at).wait()
        value = jnp.dot(
            row_loads[:, held:], ring[at % slots], preferred_element_type=jnp.float32
        )
        if at + slots < count:
            fetch(at + slots).start()
        out_ref = out_refs[at // per_out]
        place = at % per_out
        out_ref[:, place * chunk : (place + 1) * chunk] = (
            partial[at % (AHEAD + 1)] + value[:ROWS]
        ).astype(out_ref.dtype)
    yield


def first_kernel(
    orders,
    offsets,
    place_ref,
    own_ref,
    partner_ref,
    spill_a_ref,
    spill_b_ref,
    far_same_ref,
    far_cross_ref,
    *rest,
):
    held_refs = rest[:-9]
    _, inverse_ref, row_loads, *out_refs, partial, ring, sems = rest[-9:]
    tpb = partner_ref.shape[0]
    spilled = spill_a_ref.shape[0]
    even = place_ref[3] == 0
    steps = multiply(
        orders,
        place_ref[2],
        row_loads,
        held_refs,
        inverse_ref,
        out_refs,
        partial,
        ring,
        sems,
    )
    next(steps)
    for tile in range(tpb):
        total = own_ref[tile] + partner_ref[tile]
        if tile < spilled:
            total = total + jnp.where(even, spill_a_ref[tile], spill_b_ref[tile])
        if tile == offsets[0]:
            total = total + jnp.where(even, far_same_ref[0], far_cross_ref[0])
        if tile == offsets[1]:
            total = total + jnp.where(even, far_cross_ref[0], far_same_ref[0])
        both = jnp.concatenate([total, jnp.zeros_like(total)], axis=0)
        row_loads[:, tile * CT : (tile + 1) * CT] = both.astype(jnp.bfloat16)
    next(steps)


def near_kernel(count, place_ref, row_loads, *rest):
    *held_refs, near_ref, out_ref = rest
    held = len(held_refs) * PIECE
    chunk = near_ref.shape[1] // count
    for at in range(count):
        place = slice(at * chunk, (at + 1) * chunk)
        columns = pl.ds(chunk_start(place_ref[2], 0, at, chunk), chunk)
        value = held_part(row_loads, held_refs, columns)
        value = value + jnp.dot(
            row_loads[:, held:], near_ref[:, place], preferred_element_type=jnp.float32
        )[:ROWS]
        out_ref[:, place] = value


def product_stage(kernel, small, pinned, rest, outs, scratch, name):
    return pl.pallas_call(
        kernel,
        out_shape=outs,
        in_specs=[smem()] + [vmem()] * (len(small) - 1 + len(pinned)) + [anywhere()] * len(rest),
        out_specs=[vmem()] * len(outs),
        scratch_shapes=scratch,
        compiler_params=pltpu.CompilerParams(vmem_limit_bytes=PRODUCT_MIB * MIB),
        cost_estimate=pl.CostEstimate(
            flops=16 * 2048 * 4096, bytes_accessed=16 * MIB, transcendentals=0
        ),
        name=name,
    )(*small, *[pltpu.with_memory_space_constraint(piece, pltpu.VMEM) for piece in pinned], *rest)


def local(wide, narrow, sensitivity, vol_coord, ctl_coord, pair_list, pair_count, inverse):
    devices = wide * narrow
    components = sensitivity.shape[0]
    ctiles = ctl_coord.shape[1] // CT
    row_count, columns = inverse.shape
    tpb = row_count // CT
    offsets = [
        max((w * narrow + n) * ctiles // devices - w * tpb for w in range(wide))
        for n in range(narrow)
    ]
    tiles = max(offsets) + BAND
    w = lax.axis_index("wide")
    n = lax.axis_index("narrow")
    me = w * narrow + n
    far_tile = (me + devices // 2) % devices * ctiles // devices
    place = jnp.stack([w * tpb, far_tile, w, n]).astype(jnp.int32)
    geometry = (ctiles, tpb, tiles)

    chunk = columns // wide
    fast = (
        narrow == 2
        and wide >= 8
        and wide & (wide - 1) == 0
        and chunk % CT == 0
        and tiles <= 2 * tpb
        and max(offsets[0] + BAND, 0) <= tpb
        and row_count == 8 * PIECE
    )
    if not fast:
        own, spill, far_tile_loads = pair_stage(
            geometry, 0, (), pair_list, pair_count, place, sensitivity, vol_coord, ctl_coord, inverse
        )
        spans = -(-tiles // tpb)
        band = jnp.pad(spill, ((0, spans * tpb - tiles), (0, 0), (0, 0)))
        block = own
        for shift in range(1, spans):
            part = band[(shift - 1) * tpb : shift * tpb]
            block = block + lax.ppermute(
                part, "wide", [(at, (at + shift) % wide) for at in range(wide)]
            )
        far_row = far_tile % tpb
        far = jnp.zeros((tpb, ROWS, CT), jnp.float32)
        far = lax.dynamic_update_slice(far, far_tile_loads, (far_row, 0, 0))
        far_shift = wide // 2
        block = block + lax.ppermute(
            far, "wide", [(at, (at + far_shift) % wide) for at in range(wide)]
        )
        block = lax.psum(block, "narrow")
        row_loads = block.transpose(1, 0, 2).reshape(ROWS, row_count)[:components]
        terms = jnp.dot(
            row_loads.astype(jnp.bfloat16), inverse, preferred_element_type=jnp.float32
        )
        return lax.psum_scatter(terms, "wide", scatter_dimension=1, tiled=True)

    ends = range(wide // 4)
    streamed = row_count - HELD * PIECE
    own, spill, far, *pinned = pair_stage(
        geometry,
        HELD,
        (len(ends), streamed, chunk),
        pair_list,
        pair_count,
        place,
        sensitivity,
        vol_coord,
        ctl_coord,
        inverse,
    )
    held, near = pinned[:HELD], pinned[HELD:]
    both = ("wide", "narrow")
    partner = lax.ppermute(own, "narrow", [(0, 1), (1, 0)])

    def index(at_w, at_n):
        return (at_w % wide) * narrow + at_n

    spans = range(wide)
    half = wide // 2
    straight = [lambda at, k=k: (at, (at + k) % wide) for k in (1, half)]
    cross = [
        [(index(at, k), index(at + shift, 1 - k)) for at in spans for k in range(2)]
        for shift in (1, half)
    ]
    spill_b = lax.ppermute(spill, "wide", [straight[0](at) for at in spans])
    spill_a = lax.ppermute(spill, both, cross[0])
    far_same = lax.ppermute(far, "wide", [straight[1](at) for at in spans])
    far_cross = lax.ppermute(far, both, cross[1])
    quarter = columns // 4
    orders = [(difference, end) for difference in (3, 2, 1) for end in ends]
    parts = product_stage(
        functools.partial(first_kernel, orders, offsets),
        [place, own, partner, spill_a, spill_b, far_same, far_cross],
        held + near,
        [inverse],
        [
            pltpu.VMEM((2 * ROWS, row_count), jnp.bfloat16),
            jax.ShapeDtypeStruct((ROWS, quarter), jnp.bfloat16),
            jax.ShapeDtypeStruct((ROWS, quarter), jnp.bfloat16),
            jax.ShapeDtypeStruct((ROWS, quarter), jnp.float32),
        ],
        [
            pltpu.VMEM((AHEAD + 1, ROWS, chunk), jnp.float32),
            pltpu.VMEM((SLOTS, streamed, chunk), inverse.dtype),
            pltpu.SemaphoreType.DMA((SLOTS,)),
        ],
        "product_a",
    )
    row_loads = parts[0]
    moved = [
        lax.ppermute(part, "wide", [(at, at ^ difference) for at in spans])
        for part, difference in zip(parts[1:], (3, 2, 1))
    ]
    (total,) = product_stage(
        functools.partial(near_kernel, len(ends)),
        [place, row_loads],
        held + near,
        [],
        [jax.ShapeDtypeStruct((ROWS, quarter), jnp.float32)],
        [],
        "product_b",
    )
    for part in moved:
        total = total + part.astype(jnp.float32)
    result = total[:, :chunk]
    for end in ends[1:]:
        sent = total[:, end * chunk : (end + 1) * chunk].astype(jnp.bfloat16)
        got = lax.ppermute(sent, "wide", [(at, at ^ (end << 2)) for at in spans])
        result = result + got.astype(jnp.float32)
    return result[:components]


def solution(mesh):
    return jax.shard_map(
        functools.partial(local, mesh.shape["wide"], mesh.shape["narrow"]),
        mesh=mesh,
        in_specs=(
            P(None, ("wide", "narrow")),
            P(None, ("wide", "narrow")),
            P(),
            P(None, ("wide", "narrow")),
            P(("wide", "narrow")),
            P("wide", "narrow"),
        ),
        out_specs=P(None, ("narrow", "wide")),
        check_vma=False,
    )
```

```python
import functools

import jax
import jax.numpy as jnp
from jax import lax
from jax.experimental import pallas as pl
from jax.experimental.pallas import tpu as pltpu
from jax.sharding import PartitionSpec as P

CT = 128
VT = 128
BAND = 16
UNROLL = 4
AHEAD = 4
ROWS = 8
DEPTH = 64
MIB = 1 << 20
PIECE = 256
HELD = 4
SLOTS = 4
PRODUCT_MIB = 9


def thirds(value):
    high = value.astype(jnp.bfloat16).astype(jnp.float32)
    rest = value - high
    middle = rest.astype(jnp.bfloat16).astype(jnp.float32)
    return high, middle, rest - middle


def features(coords, is_node):
    width = coords.shape[1]
    scaled = 4.0 * coords - 2.0
    norm = scaled[0:1] * scaled[0:1] + scaled[1:2] * scaled[1:2] + scaled[2:3] * scaled[2:3]
    padded = jnp.concatenate([scaled, jnp.zeros((ROWS - 3, width), jnp.float32)], axis=0)
    high, middle, low = thirds(padded)
    row = lax.broadcasted_iota(jnp.int32, (ROWS, width), 0)
    n_high, n_middle, n_low = thirds(jnp.broadcast_to(norm, (ROWS, width)))
    first = 0 if is_node else 3
    norms = jnp.where(
        row == first,
        n_high,
        jnp.where(row == first + 1, n_middle, jnp.where(row == first + 2, n_low, 0.0)),
    )
    ones = jnp.where((row >= 3 - first) & (row < 6 - first), 1.0, 0.0)
    last = norms + ones
    if is_node:
        parts = [high, high, middle, middle, high, low, last]
    else:
        parts = [high, middle, high, middle, low, high]
        parts = [-2.0 * part for part in parts] + [last]
    parts = parts + [jnp.zeros((DEPTH - ROWS * len(parts), width), jnp.float32)]
    return jnp.concatenate(parts, axis=0)


def chunk_start(me, near, far, chunk):
    return pl.multiple_of((me ^ (near | (far << 2))) * chunk, chunk)


def held_copies(me, inverse_ref, held_refs, near_refs, sems=None):
    copies = []
    for at, held_ref in enumerate(held_refs):
        rows = pl.ds(at * PIECE, PIECE)
        copies.append(pltpu.make_async_copy(inverse_ref.at[rows, :], held_ref, sems.at[at]))
    for near_ref in near_refs:
        depth, width = near_ref.shape
        rows = pl.ds(len(held_refs) * PIECE, depth)
        pieces = sems.shape[0] - len(held_refs)
        chunk = width // pieces
        for at in range(pieces):
            columns = pl.ds(chunk_start(me, 0, at, chunk), chunk)
            copies.append(
                pltpu.make_async_copy(
                    inverse_ref.at[rows, columns],
                    near_ref.at[:, pl.ds(at * chunk, chunk)],
                    sems.at[len(held_refs) + at],
                )
            )
    return copies


def pair_kernel(
    geometry,
    held_count,
    near_count,
    count_ref,
    place_ref,
    listed_ref,
    sens_ref,
    vol_ref,
    ctl_ref,
    inverse_ref,
    own_ref,
    spill_ref,
    far_ref,
    *rest,
):
    ctiles, tpb, tiles = geometry
    held_refs, rest = rest[:held_count], rest[held_count:]
    near_refs, rest = rest[:near_count], rest[near_count:]
    nodes, points, weights, loads_ref, squares, kernels, sens_in, vol_in, ctl_in, list_ref, in_sems = (
        rest[:11]
    )
    vtiles = vol_ref.shape[1] // VT
    slots = list_ref.shape[1]
    inputs = [
        pltpu.make_async_copy(source, target, in_sems.at[at])
        for at, (source, target) in enumerate(
            [
                (vol_ref, vol_in),
                (ctl_ref, ctl_in),
                (sens_ref, sens_in),
                (listed_ref, list_ref),
            ]
        )
    ]
    for copy in inputs:
        copy.start()
    copies = held_copies(place_ref[2], inverse_ref, held_refs, near_refs, *rest[11:])

    first_tile = place_ref[0]
    far_tile = place_ref[1]

    loads_ref[...] = jnp.zeros(loads_ref.shape, jnp.float32)
    squares[...] = jnp.zeros(squares.shape, jnp.float32)
    kernels[...] = jnp.zeros(kernels.shape, jnp.bfloat16)
    weights[vtiles] = jnp.zeros(weights.shape[1:], jnp.bfloat16)
    for copy in inputs:
        copy.wait()
    for copy in copies:
        copy.start()

    group = 8
    square = (VT, VT)
    same = lax.broadcasted_iota(jnp.int32, square, 0) == lax.broadcasted_iota(jnp.int32, square, 1)
    unit = jnp.where(same, 1.0, 0.0).astype(jnp.bfloat16)

    def node_group(group_id, carry):
        begin = pl.multiple_of(group_id * (group * VT), group * VT)
        rows = features(vol_in[:, pl.ds(begin, group * VT)], True).astype(jnp.bfloat16)
        sens = sens_in[:, pl.ds(begin, group * VT)]
        components = sens.shape[0]
        if components < ROWS:
            sens = jnp.concatenate(
                [sens, jnp.zeros((ROWS - components, group * VT), jnp.float32)], axis=0
            )
        high = sens.astype(jnp.bfloat16).astype(jnp.float32)
        both = jnp.concatenate([high, sens - high], axis=0).astype(jnp.bfloat16)
        for at in range(group):
            cut = slice(at * VT, (at + 1) * VT)
            turned = lax.dot_general(
                unit, rows[:, cut], (((1,), (1,)), ((), ())), preferred_element_type=jnp.float32
            )
            nodes[group_id * group + at] = turned.astype(jnp.bfloat16)
            weights[group_id * group + at] = jnp.concatenate([both[:, cut], both[:, cut]], axis=1)
        return carry

    lax.fori_loop(0, vtiles // group, node_group, 0)

    for tile in range(tiles + 1):
        named = lax.rem(first_tile + tile, ctiles) if tile < tiles else far_tile
        begin = pl.multiple_of(named * CT, CT)
        points[tile] = features(ctl_in[:, pl.ds(begin, CT)], False).astype(jnp.bfloat16)

    count = count_ref[0]

    def tiles_of(slot):
        live = (slot >= 0) & (slot < count)
        at = jnp.minimum(jnp.maximum(slot, 0), slots - 1)
        volume = jnp.where(live, list_ref[0, at], 0)
        control = list_ref[1, at] - first_tile
        control = jnp.where(control < 0, control + ctiles, control)
        control = jnp.where(slot == 0, tiles, control)
        control = jnp.where(live, control, 0)
        return live, volume, control

    def pairs_step(step_id, carry):
        results = []
        for at in range(UNROLL):
            if at % 2 == 0:
                controls, pair_weights = [], []
                for slot in ((step_id - 2) * UNROLL + at, (step_id - 2) * UNROLL + at + 1):
                    live, volume, control = tiles_of(slot)
                    pair_weights.append(weights[jnp.where(live, volume, vtiles)])
                    controls.append(control)
                terms = jnp.dot(
                    jnp.concatenate(pair_weights, axis=0),
                    kernels[at // 2],
                    preferred_element_type=jnp.float32,
                )
                results.append((controls[0], terms[:ROWS, :CT] + terms[ROWS : 2 * ROWS, :CT]))
                results.append((controls[1], terms[2 * ROWS : 3 * ROWS, CT:] + terms[3 * ROWS :, CT:]))
            squared = jnp.maximum(squares[at], 1e-12)
            radius = squared * lax.rsqrt(squared)
            inside = jnp.maximum(4.0 - radius, 0.0)
            inside = inside * inside
            kernel = inside * inside * (radius + 1.0)
            high = kernel.astype(jnp.bfloat16)
            place = slice((at % 2) * CT, (at % 2 + 1) * CT)
            kernels[at // 2, :VT, place] = high
            kernels[at // 2, VT:, place] = (kernel - high.astype(jnp.float32)).astype(jnp.bfloat16)
            _, volume, control = tiles_of(step_id * UNROLL + at)
            squares[at] = jnp.dot(
                nodes[volume], points[control], preferred_element_type=jnp.float32
            )
        for control, terms in results:
            loads_ref[control] = loads_ref[control] + terms
        return carry

    lax.fori_loop(0, (count + UNROLL - 1) // UNROLL + 2, pairs_step, 0)
    own_ref[...] = loads_ref[:tpb] * (1.0 / 256.0)
    spill_ref[...] = loads_ref[tpb:tiles] * (1.0 / 256.0)
    far_ref[...] = loads_ref[tiles:] * (1.0 / 256.0)
    for copy in copies:
        copy.wait()


def vmem(shape=None):
    return pl.BlockSpec(memory_space=pltpu.VMEM)


def smem():
    return pl.BlockSpec(memory_space=pltpu.SMEM)


def anywhere():
    return pl.BlockSpec(memory_space=pltpu.HBM)


def pair_stage(geometry, held_count, near_shape, pair_list, pair_count, place, sens, vol, ctl, inverse):
    ctiles, tpb, tiles = geometry
    vtiles = vol.shape[1] // VT
    columns = inverse.shape[1]
    out_shape = [
        jax.ShapeDtypeStruct((count, ROWS, CT), jnp.float32) for count in (tpb, tiles - tpb, 1)
    ]
    out_specs = [vmem()] * 3
    scratch = [
        pltpu.VMEM((vtiles, VT, DEPTH), jnp.bfloat16),
        pltpu.VMEM((tiles + 1, DEPTH, CT), jnp.bfloat16),
        pltpu.VMEM((vtiles + 1, 2 * ROWS, 2 * VT), jnp.bfloat16),
        pltpu.VMEM((tiles + 1, ROWS, CT), jnp.float32),
        pltpu.VMEM((UNROLL, VT, CT), jnp.float32),
        pltpu.VMEM((UNROLL // 2, 2 * VT, 2 * CT), jnp.bfloat16),
        pltpu.VMEM(sens.shape, jnp.float32),
        pltpu.VMEM(vol.shape, jnp.float32),
        pltpu.VMEM(ctl.shape, jnp.float32),
        pltpu.SMEM(pair_list.shape, jnp.int32),
        pltpu.SemaphoreType.DMA((4,)),
    ]
    if held_count:
        out_shape += [pltpu.VMEM((PIECE, columns), inverse.dtype)] * held_count
        out_specs += [vmem()] * held_count
        pieces, depth, width = near_shape
        out_shape.append(pltpu.VMEM((depth, pieces * width), inverse.dtype))
        out_specs.append(vmem())
        scratch.append(pltpu.SemaphoreType.DMA((held_count + pieces,)))
    return pl.pallas_call(
        functools.partial(pair_kernel, geometry, held_count, 1 if held_count else 0),
        out_shape=out_shape,
        in_specs=[smem(), smem()] + [anywhere()] * 5,
        out_specs=out_specs,
        scratch_shapes=scratch,
        compiler_params=pltpu.CompilerParams(vmem_limit_bytes=10 * MIB),
        cost_estimate=pl.CostEstimate(
            flops=512 * 16384 * 400, bytes_accessed=held_count * PIECE * columns * 2, transcendentals=0
        ),
        name="pairs",
    )(
        pair_count,
        place,
        *[pltpu.with_memory_space_constraint(x, pltpu.HBM) for x in (pair_list, sens, vol, ctl)],
        inverse,
    )


def held_part(row_loads, held_refs, columns):
    value = jnp.zeros((2 * ROWS, columns.size), jnp.float32)
    for piece, held_ref in enumerate(held_refs):
        value = value + jnp.dot(
            row_loads[:, piece * PIECE : (piece + 1) * PIECE],
            held_ref[:, columns],
            preferred_element_type=jnp.float32,
        )
    return value[:ROWS]


def multiply(orders, me, row_loads, held_refs, inverse_ref, out_refs, partial, ring, sems):
    slots, streamed, chunk = ring.shape
    held = inverse_ref.shape[0] - streamed
    count = len(orders)
    per_out = count // len(out_refs)

    def columns_of(at):
        return pl.ds(chunk_start(me, *orders[at], chunk), chunk)

    def fetch(at):
        return pltpu.make_async_copy(
            inverse_ref.at[pl.ds(held, streamed), columns_of(at)],
            ring.at[at % slots],
            sems.at[at % slots],
        )

    for at in range(slots):
        fetch(at).start()
    yield
    for at in range(AHEAD):
        partial[at] = held_part(row_loads, held_refs, columns_of(at))
    for at in range(count):
        if at + AHEAD < count:
            partial[(at + AHEAD) % (AHEAD + 1)] = held_part(
                row_loads, held_refs, columns_of(at + AHEAD)
            )
        fetch(at).wait()
        value = jnp.dot(
            row_loads[:, held:], ring[at % slots], preferred_element_type=jnp.float32
        )
        if at + slots < count:
            fetch(at + slots).start()
        out_ref = out_refs[at // per_out]
        place = at % per_out
        out_ref[:, place * chunk : (place + 1) * chunk] = (
            partial[at % (AHEAD + 1)] + value[:ROWS]
        ).astype(out_ref.dtype)
    yield


def first_kernel(
    orders,
    offsets,
    place_ref,
    own_ref,
    partner_ref,
    spill_a_ref,
    spill_b_ref,
    far_same_ref,
    far_cross_ref,
    *rest,
):
    held_refs = rest[:-9]
    _, inverse_ref, row_loads, *out_refs, partial, ring, sems = rest[-9:]
    tpb = partner_ref.shape[0]
    spilled = spill_a_ref.shape[0]
    even = place_ref[3] == 0
    steps = multiply(
        orders,
        place_ref[2],
        row_loads,
        held_refs,
        inverse_ref,
        out_refs,
        partial,
        ring,
        sems,
    )
    next(steps)
    for tile in range(tpb):
        total = own_ref[tile] + partner_ref[tile]
        if tile < spilled:
            total = total + jnp.where(even, spill_a_ref[tile], spill_b_ref[tile])
        if tile == offsets[0]:
            total = total + jnp.where(even, far_same_ref[0], far_cross_ref[0])
        if tile == offsets[1]:
            total = total + jnp.where(even, far_cross_ref[0], far_same_ref[0])
        both = jnp.concatenate([total, jnp.zeros_like(total)], axis=0)
        row_loads[:, tile * CT : (tile + 1) * CT] = both.astype(jnp.bfloat16)
    next(steps)


def near_kernel(count, place_ref, row_loads, *rest):
    *held_refs, near_ref, out_ref = rest
    held = len(held_refs) * PIECE
    chunk = near_ref.shape[1] // count
    for at in range(count):
        place = slice(at * chunk, (at + 1) * chunk)
        columns = pl.ds(chunk_start(place_ref[2], 0, at, chunk), chunk)
        value = held_part(row_loads, held_refs, columns)
        value = value + jnp.dot(
            row_loads[:, held:], near_ref[:, place], preferred_element_type=jnp.float32
        )[:ROWS]
        out_ref[:, place] = value


def product_stage(kernel, small, pinned, rest, outs, scratch, name):
    return pl.pallas_call(
        kernel,
        out_shape=outs,
        in_specs=[smem()] + [vmem()] * (len(small) - 1 + len(pinned)) + [anywhere()] * len(rest),
        out_specs=[vmem()] * len(outs),
        scratch_shapes=scratch,
        compiler_params=pltpu.CompilerParams(vmem_limit_bytes=PRODUCT_MIB * MIB),
        cost_estimate=pl.CostEstimate(
            flops=16 * 2048 * 4096, bytes_accessed=16 * MIB, transcendentals=0
        ),
        name=name,
    )(*small, *[pltpu.with_memory_space_constraint(piece, pltpu.VMEM) for piece in pinned], *rest)


def local(wide, narrow, sensitivity, vol_coord, ctl_coord, pair_list, pair_count, inverse):
    devices = wide * narrow
    components = sensitivity.shape[0]
    ctiles = ctl_coord.shape[1] // CT
    row_count, columns = inverse.shape
    tpb = row_count // CT
    offsets = [
        max((w * narrow + n) * ctiles // devices - w * tpb for w in range(wide))
        for n in range(narrow)
    ]
    tiles = max(offsets) + BAND
    w = lax.axis_index("wide")
    n = lax.axis_index("narrow")
    me = w * narrow + n
    far_tile = (me + devices // 2) % devices * ctiles // devices
    place = jnp.stack([w * tpb, far_tile, w, n]).astype(jnp.int32)
    geometry = (ctiles, tpb, tiles)

    chunk = columns // wide
    fast = (
        narrow == 2
        and wide >= 8
        and wide & (wide - 1) == 0
        and chunk % CT == 0
        and tiles <= 2 * tpb
        and max(offsets[0] + BAND, 0) <= tpb
        and row_count == 8 * PIECE
    )
    if not fast:
        own, spill, far_tile_loads = pair_stage(
            geometry, 0, (), pair_list, pair_count, place, sensitivity, vol_coord, ctl_coord, inverse
        )
        spans = -(-tiles // tpb)
        band = jnp.pad(spill, ((0, spans * tpb - tiles), (0, 0), (0, 0)))
        block = own
        for shift in range(1, spans):
            part = band[(shift - 1) * tpb : shift * tpb]
            block = block + lax.ppermute(
                part, "wide", [(at, (at + shift) % wide) for at in range(wide)]
            )
        far_row = far_tile % tpb
        far = jnp.zeros((tpb, ROWS, CT), jnp.float32)
        far = lax.dynamic_update_slice(far, far_tile_loads, (far_row, 0, 0))
        far_shift = wide // 2
        block = block + lax.ppermute(
            far, "wide", [(at, (at + far_shift) % wide) for at in range(wide)]
        )
        block = lax.psum(block, "narrow")
        row_loads = block.transpose(1, 0, 2).reshape(ROWS, row_count)[:components]
        terms = jnp.dot(
            row_loads.astype(jnp.bfloat16), inverse, preferred_element_type=jnp.float32
        )
        return lax.psum_scatter(terms, "wide", scatter_dimension=1, tiled=True)

    ends = range(wide // 4)
    streamed = row_count - HELD * PIECE
    own, spill, far, *pinned = pair_stage(
        geometry,
        HELD,
        (len(ends), streamed, chunk),
        pair_list,
        pair_count,
        place,
        sensitivity,
        vol_coord,
        ctl_coord,
        inverse,
    )
    held, near = pinned[:HELD], pinned[HELD:]
    both = ("wide", "narrow")
    partner = lax.ppermute(own, "narrow", [(0, 1), (1, 0)])

    def index(at_w, at_n):
        return (at_w % wide) * narrow + at_n

    spans = range(wide)
    half = wide // 2
    straight = [lambda at, k=k: (at, (at + k) % wide) for k in (1, half)]
    cross = [
        [(index(at, k), index(at + shift, 1 - k)) for at in spans for k in range(2)]
        for shift in (1, half)
    ]
    spill_b = lax.ppermute(spill, "wide", [straight[0](at) for at in spans])
    spill_a = lax.ppermute(spill, both, cross[0])
    far_same = lax.ppermute(far, "wide", [straight[1](at) for at in spans])
    far_cross = lax.ppermute(far, both, cross[1])
    quarter = columns // 4
    orders = [(difference, end) for difference in (3, 2, 1) for end in ends]
    parts = product_stage(
        functools.partial(first_kernel, orders, offsets),
        [place, own, partner, spill_a, spill_b, far_same, far_cross],
        held + near,
        [inverse],
        [
            pltpu.VMEM((2 * ROWS, row_count), jnp.bfloat16),
            jax.ShapeDtypeStruct((ROWS, quarter), jnp.bfloat16),
            jax.ShapeDtypeStruct((ROWS, quarter), jnp.bfloat16),
            jax.ShapeDtypeStruct((ROWS, quarter), jnp.float32),
        ],
        [
            pltpu.VMEM((AHEAD + 1, ROWS, chunk), jnp.float32),
            pltpu.VMEM((SLOTS, streamed, chunk), inverse.dtype),
            pltpu.SemaphoreType.DMA((SLOTS,)),
        ],
        "product_a",
    )
    row_loads = parts[0]
    moved = [
        lax.ppermute(part, "wide", [(at, at ^ difference) for at in spans])
        for part, difference in zip(parts[1:], (3, 2, 1))
    ]
    (total,) = product_stage(
        functools.partial(near_kernel, len(ends)),
        [place, row_loads],
        held + near,
        [],
        [jax.ShapeDtypeStruct((ROWS, quarter), jnp.float32)],
        [],
        "product_b",
    )
    for part in moved:
        total = total + part.astype(jnp.float32)
    result = total[:, :chunk]
    for end in ends[1:]:
        sent = total[:, end * chunk : (end + 1) * chunk].astype(jnp.bfloat16)
        got = lax.ppermute(sent, "wide", [(at, at ^ (end << 2)) for at in spans])
        result = result + got.astype(jnp.float32)
    return result[:components]


def solution(mesh):
    return jax.shard_map(
        functools.partial(local, mesh.shape["wide"], mesh.shape["narrow"]),
        mesh=mesh,
        in_specs=(
            P(None, ("wide", "narrow")),
            P(None, ("wide", "narrow")),
            P(),
            P(None, ("wide", "narrow")),
            P(("wide", "narrow")),
            P("wide", "narrow"),
        ),
        out_specs=P(None, ("narrow", "wide")),
        check_vma=False,
    )
```

```python
import functools

import jax
import jax.numpy as jnp
from jax import lax
from jax.experimental import pallas as pl
from jax.experimental.pallas import tpu as pltpu
from jax.sharding import PartitionSpec as P

CT = 128
VT = 128
BAND = 16
UNROLL = 16
AHEAD = 4
ROWS = 8
DEPTH = 64
MIB = 1 << 20
PIECE = 256
HELD = 4
SLOTS = 4
PRODUCT_MIB = 9


def thirds(value):
    high = value.astype(jnp.bfloat16).astype(jnp.float32)
    rest = value - high
    middle = rest.astype(jnp.bfloat16).astype(jnp.float32)
    return high, middle, rest - middle


def features(coords, is_node):
    width = coords.shape[1]
    scaled = 4.0 * coords - 2.0
    norm = scaled[0:1] * scaled[0:1] + scaled[1:2] * scaled[1:2] + scaled[2:3] * scaled[2:3]
    padded = jnp.concatenate([scaled, jnp.zeros((ROWS - 3, width), jnp.float32)], axis=0)
    high, middle, low = thirds(padded)
    row = lax.broadcasted_iota(jnp.int32, (ROWS, width), 0)
    n_high, n_middle, n_low = thirds(jnp.broadcast_to(norm, (ROWS, width)))
    first = 0 if is_node else 3
    norms = jnp.where(
        row == first,
        n_high,
        jnp.where(row == first + 1, n_middle, jnp.where(row == first + 2, n_low, 0.0)),
    )
    ones = jnp.where((row >= 3 - first) & (row < 6 - first), 1.0, 0.0)
    last = norms + ones
    if is_node:
        parts = [high, high, middle, middle, high, low, last]
    else:
        parts = [high, middle, high, middle, low, high]
        parts = [-2.0 * part for part in parts] + [last]
    parts = parts + [jnp.zeros((DEPTH - ROWS * len(parts), width), jnp.float32)]
    return jnp.concatenate(parts, axis=0)


def chunk_start(me, near, far, chunk):
    return pl.multiple_of((me ^ (near | (far << 2))) * chunk, chunk)


def held_copies(me, inverse_ref, held_refs, near_refs, sems=None):
    copies = []
    for at, held_ref in enumerate(held_refs):
        rows = pl.ds(at * PIECE, PIECE)
        copies.append(pltpu.make_async_copy(inverse_ref.at[rows, :], held_ref, sems.at[at]))
    for near_ref in near_refs:
        depth, width = near_ref.shape
        rows = pl.ds(len(held_refs) * PIECE, depth)
        pieces = sems.shape[0] - len(held_refs)
        chunk = width // pieces
        for at in range(pieces):
            columns = pl.ds(chunk_start(me, 0, at, chunk), chunk)
            copies.append(
                pltpu.make_async_copy(
                    inverse_ref.at[rows, columns],
                    near_ref.at[:, pl.ds(at * chunk, chunk)],
                    sems.at[len(held_refs) + at],
                )
            )
    return copies


def pair_kernel(
    geometry,
    held_count,
    near_count,
    count_ref,
    place_ref,
    listed_ref,
    sens_ref,
    vol_ref,
    ctl_ref,
    inverse_ref,
    own_ref,
    spill_ref,
    far_ref,
    *rest,
):
    ctiles, tpb, tiles = geometry
    held_refs, rest = rest[:held_count], rest[held_count:]
    near_refs, rest = rest[:near_count], rest[near_count:]
    nodes, points, weights, loads_ref, squares, kernels, sens_in, vol_in, ctl_in, list_ref, in_sems = (
        rest[:11]
    )
    vtiles = vol_ref.shape[1] // VT
    slots = list_ref.shape[1]
    inputs = [
        pltpu.make_async_copy(source, target, in_sems.at[at])
        for at, (source, target) in enumerate(
            [
                (vol_ref, vol_in),
                (ctl_ref, ctl_in),
                (sens_ref, sens_in),
                (listed_ref, list_ref),
            ]
        )
    ]
    for copy in inputs:
        copy.start()
    copies = held_copies(place_ref[2], inverse_ref, held_refs, near_refs, *rest[11:])

    first_tile = place_ref[0]
    far_tile = place_ref[1]

    loads_ref[...] = jnp.zeros(loads_ref.shape, jnp.float32)
    squares[...] = jnp.zeros(squares.shape, jnp.float32)
    kernels[...] = jnp.zeros(kernels.shape, jnp.bfloat16)
    weights[vtiles] = jnp.zeros(weights.shape[1:], jnp.bfloat16)
    for copy in inputs:
        copy.wait()
    for copy in copies:
        copy.start()

    group = 8
    square = (VT, VT)
    same = lax.broadcasted_iota(jnp.int32, square, 0) == lax.broadcasted_iota(jnp.int32, square, 1)
    unit = jnp.where(same, 1.0, 0.0).astype(jnp.bfloat16)

    def node_group(group_id, carry):
        begin = pl.multiple_of(group_id * (group * VT), group * VT)
        rows = features(vol_in[:, pl.ds(begin, group * VT)], True).astype(jnp.bfloat16)
        sens = sens_in[:, pl.ds(begin, group * VT)]
        components = sens.shape[0]
        if components < ROWS:
            sens = jnp.concatenate(
                [sens, jnp.zeros((ROWS - components, group * VT), jnp.float32)], axis=0
            )
        high = sens.astype(jnp.bfloat16).astype(jnp.float32)
        both = jnp.concatenate([high, sens - high], axis=0).astype(jnp.bfloat16)
        for at in range(group):
            cut = slice(at * VT, (at + 1) * VT)
            turned = lax.dot_general(
                unit, rows[:, cut], (((1,), (1,)), ((), ())), preferred_element_type=jnp.float32
            )
            nodes[group_id * group + at] = turned.astype(jnp.bfloat16)
            weights[group_id * group + at] = jnp.concatenate([both[:, cut], both[:, cut]], axis=1)
        return carry

    lax.fori_loop(0, vtiles // group, node_group, 0)

    for tile in range(tiles + 1):
        named = lax.rem(first_tile + tile, ctiles) if tile < tiles else far_tile
        begin = pl.multiple_of(named * CT, CT)
        points[tile] = features(ctl_in[:, pl.ds(begin, CT)], False).astype(jnp.bfloat16)

    count = count_ref[0]

    def tiles_of(slot):
        live = (slot >= 0) & (slot < count)
        at = jnp.minimum(jnp.maximum(slot, 0), slots - 1)
        volume = jnp.where(live, list_ref[0, at], 0)
        control = list_ref[1, at] - first_tile
        control = jnp.where(control < 0, control + ctiles, control)
        control = jnp.where(slot == 0, tiles, control)
        control = jnp.where(live, control, 0)
        return live, volume, control

    def pairs_step(step_id, carry):
        results = []
        for at in range(UNROLL):
            if at % 2 == 0:
                controls, pair_weights = [], []
                for slot in ((step_id - 2) * UNROLL + at, (step_id - 2) * UNROLL + at + 1):
                    live, volume, control = tiles_of(slot)
                    pair_weights.append(weights[jnp.where(live, volume, vtiles)])
                    controls.append(control)
                terms = jnp.dot(
                    jnp.concatenate(pair_weights, axis=0),
                    kernels[at // 2],
                    preferred_element_type=jnp.float32,
                )
                results.append((controls[0], terms[:ROWS, :CT] + terms[ROWS : 2 * ROWS, :CT]))
                results.append((controls[1], terms[2 * ROWS : 3 * ROWS, CT:] + terms[3 * ROWS :, CT:]))
            squared = jnp.maximum(squares[at], 1e-12)
            radius = squared * lax.rsqrt(squared)
            inside = jnp.maximum(4.0 - radius, 0.0)
            inside = inside * inside
            kernel = inside * inside * (radius + 1.0)
            high = kernel.astype(jnp.bfloat16)
            place = slice((at % 2) * CT, (at % 2 + 1) * CT)
            kernels[at // 2, :VT, place] = high
            kernels[at // 2, VT:, place] = (kernel - high.astype(jnp.float32)).astype(jnp.bfloat16)
            _, volume, control = tiles_of(step_id * UNROLL + at)
            squares[at] = jnp.dot(
                nodes[volume], points[control], preferred_element_type=jnp.float32
            )
        for control, terms in results:
            loads_ref[control] = loads_ref[control] + terms
        return carry

    lax.fori_loop(0, (count + UNROLL - 1) // UNROLL + 2, pairs_step, 0)
    own_ref[...] = loads_ref[:tpb] * (1.0 / 256.0)
    spill_ref[...] = loads_ref[tpb:tiles] * (1.0 / 256.0)
    far_ref[...] = loads_ref[tiles:] * (1.0 / 256.0)
    for copy in copies:
        copy.wait()


def vmem(shape=None):
    return pl.BlockSpec(memory_space=pltpu.VMEM)


def smem():
    return pl.BlockSpec(memory_space=pltpu.SMEM)


def anywhere():
    return pl.BlockSpec(memory_space=pltpu.HBM)


def pair_stage(geometry, held_count, near_shape, pair_list, pair_count, place, sens, vol, ctl, inverse):
    ctiles, tpb, tiles = geometry
    vtiles = vol.shape[1] // VT
    columns = inverse.shape[1]
    out_shape = [
        jax.ShapeDtypeStruct((count, ROWS, CT), jnp.float32) for count in (tpb, tiles - tpb, 1)
    ]
    out_specs = [vmem()] * 3
    scratch = [
        pltpu.VMEM((vtiles, VT, DEPTH), jnp.bfloat16),
        pltpu.VMEM((tiles + 1, DEPTH, CT), jnp.bfloat16),
        pltpu.VMEM((vtiles + 1, 2 * ROWS, 2 * VT), jnp.bfloat16),
        pltpu.VMEM((tiles + 1, ROWS, CT), jnp.float32),
        pltpu.VMEM((UNROLL, VT, CT), jnp.float32),
        pltpu.VMEM((UNROLL // 2, 2 * VT, 2 * CT), jnp.bfloat16),
        pltpu.VMEM(sens.shape, jnp.float32),
        pltpu.VMEM(vol.shape, jnp.float32),
        pltpu.VMEM(ctl.shape, jnp.float32),
        pltpu.SMEM(pair_list.shape, jnp.int32),
        pltpu.SemaphoreType.DMA((4,)),
    ]
    if held_count:
        out_shape += [pltpu.VMEM((PIECE, columns), inverse.dtype)] * held_count
        out_specs += [vmem()] * held_count
        pieces, depth, width = near_shape
        out_shape.append(pltpu.VMEM((depth, pieces * width), inverse.dtype))
        out_specs.append(vmem())
        scratch.append(pltpu.SemaphoreType.DMA((held_count + pieces,)))
    return pl.pallas_call(
        functools.partial(pair_kernel, geometry, held_count, 1 if held_count else 0),
        out_shape=out_shape,
        in_specs=[smem(), smem()] + [anywhere()] * 5,
        out_specs=out_specs,
        scratch_shapes=scratch,
        compiler_params=pltpu.CompilerParams(vmem_limit_bytes=10 * MIB),
        cost_estimate=pl.CostEstimate(
            flops=512 * 16384 * 400, bytes_accessed=held_count * PIECE * columns * 2, transcendentals=0
        ),
        name="pairs",
    )(
        pair_count,
        place,
        *[pltpu.with_memory_space_constraint(x, pltpu.HBM) for x in (pair_list, sens, vol, ctl)],
        inverse,
    )


def held_part(row_loads, held_refs, columns):
    value = jnp.zeros((2 * ROWS, columns.size), jnp.float32)
    for piece, held_ref in enumerate(held_refs):
        value = value + jnp.dot(
            row_loads[:, piece * PIECE : (piece + 1) * PIECE],
            held_ref[:, columns],
            preferred_element_type=jnp.float32,
        )
    return value[:ROWS]


def multiply(orders, me, row_loads, held_refs, inverse_ref, out_refs, partial, ring, sems):
    slots, streamed, chunk = ring.shape
    held = inverse_ref.shape[0] - streamed
    count = len(orders)
    per_out = count // len(out_refs)

    def columns_of(at):
        return pl.ds(chunk_start(me, *orders[at], chunk), chunk)

    def fetch(at):
        return pltpu.make_async_copy(
            inverse_ref.at[pl.ds(held, streamed), columns_of(at)],
            ring.at[at % slots],
            sems.at[at % slots],
        )

    for at in range(slots):
        fetch(at).start()
    yield
    for at in range(AHEAD):
        partial[at] = held_part(row_loads, held_refs, columns_of(at))
    for at in range(count):
        if at + AHEAD < count:
            partial[(at + AHEAD) % (AHEAD + 1)] = held_part(
                row_loads, held_refs, columns_of(at + AHEAD)
            )
        fetch(at).wait()
        value = jnp.dot(
            row_loads[:, held:], ring[at % slots], preferred_element_type=jnp.float32
        )
        if at + slots < count:
            fetch(at + slots).start()
        out_ref = out_refs[at // per_out]
        place = at % per_out
        out_ref[:, place * chunk : (place + 1) * chunk] = (
            partial[at % (AHEAD + 1)] + value[:ROWS]
        ).astype(out_ref.dtype)
    yield


def first_kernel(
    orders,
    offsets,
    place_ref,
    own_ref,
    partner_ref,
    spill_a_ref,
    spill_b_ref,
    far_same_ref,
    far_cross_ref,
    *rest,
):
    held_refs = rest[:-9]
    _, inverse_ref, row_loads, *out_refs, partial, ring, sems = rest[-9:]
    tpb = partner_ref.shape[0]
    spilled = spill_a_ref.shape[0]
    even = place_ref[3] == 0
    steps = multiply(
        orders,
        place_ref[2],
        row_loads,
        held_refs,
        inverse_ref,
        out_refs,
        partial,
        ring,
        sems,
    )
    next(steps)
    for tile in range(tpb):
        total = own_ref[tile] + partner_ref[tile]
        if tile < spilled:
            total = total + jnp.where(even, spill_a_ref[tile], spill_b_ref[tile])
        if tile == offsets[0]:
            total = total + jnp.where(even, far_same_ref[0], far_cross_ref[0])
        if tile == offsets[1]:
            total = total + jnp.where(even, far_cross_ref[0], far_same_ref[0])
        both = jnp.concatenate([total, jnp.zeros_like(total)], axis=0)
        row_loads[:, tile * CT : (tile + 1) * CT] = both.astype(jnp.bfloat16)
    next(steps)


def near_kernel(count, place_ref, row_loads, *rest):
    *held_refs, near_ref, out_ref = rest
    held = len(held_refs) * PIECE
    chunk = near_ref.shape[1] // count
    for at in range(count):
        place = slice(at * chunk, (at + 1) * chunk)
        columns = pl.ds(chunk_start(place_ref[2], 0, at, chunk), chunk)
        value = held_part(row_loads, held_refs, columns)
        value = value + jnp.dot(
            row_loads[:, held:], near_ref[:, place], preferred_element_type=jnp.float32
        )[:ROWS]
        out_ref[:, place] = value


def product_stage(kernel, small, pinned, rest, outs, scratch, name):
    return pl.pallas_call(
        kernel,
        out_shape=outs,
        in_specs=[smem()] + [vmem()] * (len(small) - 1 + len(pinned)) + [anywhere()] * len(rest),
        out_specs=[vmem()] * len(outs),
        scratch_shapes=scratch,
        compiler_params=pltpu.CompilerParams(vmem_limit_bytes=PRODUCT_MIB * MIB),
        cost_estimate=pl.CostEstimate(
            flops=16 * 2048 * 4096, bytes_accessed=16 * MIB, transcendentals=0
        ),
        name=name,
    )(*small, *[pltpu.with_memory_space_constraint(piece, pltpu.VMEM) for piece in pinned], *rest)


def local(wide, narrow, sensitivity, vol_coord, ctl_coord, pair_list, pair_count, inverse):
    devices = wide * narrow
    components = sensitivity.shape[0]
    ctiles = ctl_coord.shape[1] // CT
    row_count, columns = inverse.shape
    tpb = row_count // CT
    offsets = [
        max((w * narrow + n) * ctiles // devices - w * tpb for w in range(wide))
        for n in range(narrow)
    ]
    tiles = max(offsets) + BAND
    w = lax.axis_index("wide")
    n = lax.axis_index("narrow")
    me = w * narrow + n
    far_tile = (me + devices // 2) % devices * ctiles // devices
    place = jnp.stack([w * tpb, far_tile, w, n]).astype(jnp.int32)
    geometry = (ctiles, tpb, tiles)

    chunk = columns // wide
    fast = (
        narrow == 2
        and wide >= 8
        and wide & (wide - 1) == 0
        and chunk % CT == 0
        and tiles <= 2 * tpb
        and max(offsets[0] + BAND, 0) <= tpb
        and row_count == 8 * PIECE
    )
    if not fast:
        own, spill, far_tile_loads = pair_stage(
            geometry, 0, (), pair_list, pair_count, place, sensitivity, vol_coord, ctl_coord, inverse
        )
        spans = -(-tiles // tpb)
        band = jnp.pad(spill, ((0, spans * tpb - tiles), (0, 0), (0, 0)))
        block = own
        for shift in range(1, spans):
            part = band[(shift - 1) * tpb : shift * tpb]
            block = block + lax.ppermute(
                part, "wide", [(at, (at + shift) % wide) for at in range(wide)]
            )
        far_row = far_tile % tpb
        far = jnp.zeros((tpb, ROWS, CT), jnp.float32)
        far = lax.dynamic_update_slice(far, far_tile_loads, (far_row, 0, 0))
        far_shift = wide // 2
        block = block + lax.ppermute(
            far, "wide", [(at, (at + far_shift) % wide) for at in range(wide)]
        )
        block = lax.psum(block, "narrow")
        row_loads = block.transpose(1, 0, 2).reshape(ROWS, row_count)[:components]
        terms = jnp.dot(
            row_loads.astype(jnp.bfloat16), inverse, preferred_element_type=jnp.float32
        )
        return lax.psum_scatter(terms, "wide", scatter_dimension=1, tiled=True)

    ends = range(wide // 4)
    streamed = row_count - HELD * PIECE
    own, spill, far, *pinned = pair_stage(
        geometry,
        HELD,
        (len(ends), streamed, chunk),
        pair_list,
        pair_count,
        place,
        sensitivity,
        vol_coord,
        ctl_coord,
        inverse,
    )
    held, near = pinned[:HELD], pinned[HELD:]
    both = ("wide", "narrow")
    partner = lax.ppermute(own, "narrow", [(0, 1), (1, 0)])

    def index(at_w, at_n):
        return (at_w % wide) * narrow + at_n

    spans = range(wide)
    half = wide // 2
    straight = [lambda at, k=k: (at, (at + k) % wide) for k in (1, half)]
    cross = [
        [(index(at, k), index(at + shift, 1 - k)) for at in spans for k in range(2)]
        for shift in (1, half)
    ]
    spill_b = lax.ppermute(spill, "wide", [straight[0](at) for at in spans])
    spill_a = lax.ppermute(spill, both, cross[0])
    far_same = lax.ppermute(far, "wide", [straight[1](at) for at in spans])
    far_cross = lax.ppermute(far, both, cross[1])
    quarter = columns // 4
    orders = [(difference, end) for difference in (3, 2, 1) for end in ends]
    parts = product_stage(
        functools.partial(first_kernel, orders, offsets),
        [place, own, partner, spill_a, spill_b, far_same, far_cross],
        held + near,
        [inverse],
        [
            pltpu.VMEM((2 * ROWS, row_count), jnp.bfloat16),
            jax.ShapeDtypeStruct((ROWS, quarter), jnp.bfloat16),
            jax.ShapeDtypeStruct((ROWS, quarter), jnp.bfloat16),
            jax.ShapeDtypeStruct((ROWS, quarter), jnp.float32),
        ],
        [
            pltpu.VMEM((AHEAD + 1, ROWS, chunk), jnp.float32),
            pltpu.VMEM((SLOTS, streamed, chunk), inverse.dtype),
            pltpu.SemaphoreType.DMA((SLOTS,)),
        ],
        "product_a",
    )
    row_loads = parts[0]
    moved = [
        lax.ppermute(part, "wide", [(at, at ^ difference) for at in spans])
        for part, difference in zip(parts[1:], (3, 2, 1))
    ]
    (total,) = product_stage(
        functools.partial(near_kernel, len(ends)),
        [place, row_loads],
        held + near,
        [],
        [jax.ShapeDtypeStruct((ROWS, quarter), jnp.float32)],
        [],
        "product_b",
    )
    for part in moved:
        total = total + part.astype(jnp.float32)
    result = total[:, :chunk]
    for end in ends[1:]:
        sent = total[:, end * chunk : (end + 1) * chunk].astype(jnp.bfloat16)
        got = lax.ppermute(sent, "wide", [(at, at ^ (end << 2)) for at in spans])
        result = result + got.astype(jnp.float32)
    return result[:components]


def solution(mesh):
    return jax.shard_map(
        functools.partial(local, mesh.shape["wide"], mesh.shape["narrow"]),
        mesh=mesh,
        in_specs=(
            P(None, ("wide", "narrow")),
            P(None, ("wide", "narrow")),
            P(),
            P(None, ("wide", "narrow")),
            P(("wide", "narrow")),
            P("wide", "narrow"),
        ),
        out_specs=P(None, ("narrow", "wide")),
        check_vma=False,
    )
```
